256 devices in a mesh: dp: 8 (over z), vocab: 32 (over y, x, core).
Axes of the slice: x: 4, y: 4, z: 8, core: 2. Of those that a mesh axis runs over, the one named last changes fastest.
Arguments:
- hidden: bfloat16 [32768, 4096], P(('dp', 'vocab')), may hold values from -4 to 4
- output_weight: bfloat16 [4096, 32768], P(None, 'vocab'), may hold values from -0.09375 to 0.09375
- owners: int32 [32768, 3], P(('dp', 'vocab')), may hold values from 0 to 31, all different within a row; in each aligned block of 128 rows (0 to 127, 128 to 255, ...) at most 16 rows name the same one
- negatives: int32 [32768, 3, 2], P(('dp', 'vocab')), may hold values from 0 to 7
- negative_mask: int32 [32768, 3, 2], P(('dp', 'vocab')), may hold values 0 or 1
- target_block: int32 [32768], P(('dp', 'vocab')), may hold values from 0 to 7
- target_word: int32 [32768], P(('dp', 'vocab')), may hold values from 0 to 127
- log_norm: bfloat16 [32768], P(('dp', 'vocab')), may hold values from 1 to 2
- cotangent: bfloat16 [32768], P(('dp', 'vocab')), may hold values from 4 to 8
Outputs:
- hidden_grad: bfloat16 [32768, 4096], P(('dp', 'vocab'))
- weight_grad: bfloat16 [4096, 32768], P('dp', 'vocab')
The draws below stay inside these ranges and needn't reach their ends.
Inputs may be any that keep to these rules, and one draw needn't show every extreme that they name: Each row names 3 different owners; among the 128 rows of one device no owner is named by more than 16 rows, and in some device's rows an owner is named by exactly 16.
All inputs are finite; a program needn't handle non-finite values. No bound on the sum of `negative_mask` on one device may be relied on, other than what follows from the above.
Results may differ from the reference program's by a relative error of at most 0.015.
Values may be sent and summed in bfloat16 or wider, within the bound.
No kernel may reach another device: no remote copies, remote signals or barrier semaphores. Data moves between devices by JAX's collectives and lax.ppermute only.
A program may use at most 128 MiB of HBM per device.

```python
import math
import jax
import jax.numpy as jnp
import numpy as np
from jax import lax

H = 4096
BLOCK = 128
VIS = 3
PER_OWN = 2
BLK_DEV = 8
TOK_DEV = 128
CAP = 16
GROUP_TOK = 4096
TOKENS = 32768
WORDS = 32768
N_DP = 8
N_VOCAB = 32


def set_ends(values, own_key, low, high):
    longest = values.shape.index(max(values.shape))
    spots = []
    for shift in (0, 1):
        where = [jax.random.randint(jax.random.fold_in(own_key, axis), (), 0, length) for axis, length in enumerate(values.shape)]
        where[longest] = (where[longest] + shift) % values.shape[longest]
        spots.append(tuple(where))
    return values.at[spots[0]].set(low).at[spots[1]].set(high)


def block_scale(rng, dims, cuts, least, largest):
    loudness = 1.0
    for position, parts in cuts:
        heights = jax.random.uniform(jax.random.fold_in(jax.random.fold_in(rng, 6), position), (parts,), jnp.float32, least / len(cuts), largest / len(cuts))
        loudness = loudness * jnp.repeat(jnp.exp(heights), dims[position] // parts).reshape((-1,) + (1,) * (len(dims) - 1 - position))
    return loudness


def assign_block(key, own, number, rows, number_of, top, bound, skew):
    sequence = jax.random.permutation(key, number_of)
    crowded, common = load_shares(number_of, rows * top, bound, skew, True), load_shares(number_of, rows * top, bound, skew, False)
    places = jnp.arange(number_of)

    def named(lengths, turn):
        used = int((lengths > 0).sum())
        fixed = max(1, used // 4)
        shifted = fixed + (places - fixed + turn * (used - fixed)) % max(1, number_of - fixed)
        return jnp.zeros((number_of,), jnp.int32).at[sequence[jnp.where(places < fixed, places, shifted)]].set(jnp.asarray(lengths, jnp.int32))

    lengths = jnp.where(number % 4 == 0, named(crowded, number // 4), named(common, number - number // 4 - 1))
    mixed = jax.random.permutation(jax.random.fold_in(own, 3), number_of)
    giver, taker = mixed[0:number_of // 2 * 2:2], mixed[1:number_of // 2 * 2:2]
    slack = jnp.minimum(lengths[giver] - 1, bound - lengths[taker]) // 2
    slack = jnp.where((giver == sequence[0]) | (taker == sequence[0]) | (lengths[taker] == 0), 0, jnp.maximum(slack, 0))
    shifted = jax.random.randint(jax.random.fold_in(own, 4), (number_of // 2,), 0, 1 << 20) % (slack + 1)
    lengths = lengths.at[giver].add(-shifted).at[taker].add(shifted)
    items = jnp.searchsorted(jnp.cumsum(lengths), jnp.arange(rows * top), side="right").astype(jnp.int32)
    table = items.reshape(top, rows).T
    table = table[jax.random.permutation(jax.random.fold_in(own, 1), rows)]
    turn = jax.random.randint(jax.random.fold_in(own, 2), (rows, 1), 0, top)
    return jnp.take_along_axis(table, (jnp.arange(top)[None, :] + turn) % top, axis=1)


def load_shares(number_of, total, bound, slope, full):
    loads = [(1 << 20) // math.isqrt(grade ** slope) + 1 for grade in range(1, number_of + 1)]
    largest = bound if full else min(bound, max(-(-total // number_of), total * loads[0] // sum(loads)))
    least = 1 if total - largest >= number_of - 1 else 0
    counts, surplus = [largest] + [least] * (number_of - 1), total - largest - least * (number_of - 1)
    while surplus > 0:
        candidates = [i for i in range(1, number_of) if counts[i] < largest] or [i for i in range(1, number_of) if counts[i] < bound]
        whole, budget = sum([loads[i] for i in candidates]), surplus
        for i in candidates:
            more = min(bound - counts[i], max(1, budget * loads[i] // whole), surplus)
            counts[i] = counts[i] + more
            surplus = surplus - more
    return np.array(counts)


def scatter_about(rng, shape, spread, most, cuts=(), held_as=jnp.bfloat16):
    values = jax.random.normal(rng, shape, jnp.float32) * spread
    if len(cuts) > 0:
        values = block_scale(rng, shape, cuts, -0.22, 0.18) * values
    return jnp.clip(values, min=-most, max=most).astype(held_as)


def setup_inputs(seed: int = 0) -> dict:
    keys = jax.random.split(jax.random.key(seed), 10)
    hidden = scatter_about(keys[0], (TOKENS, H), 0.5, 4.0, ((0, 256),))
    output_weight = scatter_about(keys[1], (H, WORDS), H ** -0.5, 0.09375, ((1, 32),))
    owners_keys = jax.random.split(jax.random.fold_in(keys[2], 1), TOKENS // TOK_DEV)
    owners_turns = jax.random.permutation(jax.random.fold_in(keys[2], 3), TOKENS // TOK_DEV)
    owners = jax.vmap(lambda own, number: assign_block(jax.random.fold_in(keys[2], 2), own, number, TOK_DEV, N_VOCAB, VIS, CAP, 2))(owners_keys, owners_turns).reshape((TOKENS, VIS))
    negatives = set_ends(jax.random.randint(keys[3], (TOKENS, VIS, PER_OWN), 0, BLK_DEV), jax.random.fold_in(keys[3], 1), 0, BLK_DEV - 1).astype(jnp.int32)
    negative_mask = set_ends((jax.random.randint(keys[4], (TOKENS, VIS, PER_OWN), 0, 4) < 3).astype(jnp.int32), jax.random.fold_in(keys[4], 1), 0, 1)
    target_block = set_ends(jax.random.randint(keys[5], (TOKENS,), 0, BLK_DEV), jax.random.fold_in(keys[5], 1), 0, BLK_DEV - 1).astype(jnp.int32)
    target_word = set_ends(jax.random.randint(keys[6], (TOKENS,), 0, BLOCK), jax.random.fold_in(keys[6], 1), 0, BLOCK - 1).astype(jnp.int32)
    log_norm = jnp.clip(1.0 + 1.0 * jax.random.uniform(keys[7], (TOKENS,), jnp.float32) ** block_scale(keys[7], (TOKENS,), ((0, 256),), -0.2, 0.2), 1.0, 2.0).astype(jnp.bfloat16)
    cotangent = jnp.clip(4.0 + 4.0 * jax.random.uniform(keys[8], (TOKENS,), jnp.float32) ** block_scale(keys[8], (TOKENS,), ((0, 256),), -0.2, 0.2), 4.0, 8.0).astype(jnp.bfloat16)
    return dict(hidden=hidden, output_weight=output_weight, owners=owners, negatives=negatives, negative_mask=negative_mask, target_block=target_block, target_word=target_word, log_norm=log_norm, cotangent=cotangent)


def reference(hidden, output_weight, owners, negatives, negative_mask, target_block, target_word, log_norm, cotangent):
    owner_words = BLK_DEV * BLOCK
    entries = GROUP_TOK * VIS
    reach = N_VOCAB * CAP
    word_position = jnp.arange(owner_words).astype(jnp.float32)
    cluster_ids = jnp.arange(BLK_DEV).astype(jnp.int32)

    def group_step(weight_acc, group):
        first_row = group * GROUP_TOK

        def take_group(array):
            return lax.dynamic_slice_in_dim(array, first_row, GROUP_TOK, 0)

        group_hidden = take_group(hidden)
        flat_owner = take_group(owners).reshape(entries)
        group_negative = take_group(negatives).reshape(entries, PER_OWN)
        group_mask = take_group(negative_mask).reshape(entries, PER_OWN)
        group_block = take_group(target_block)
        group_word = take_group(target_word)
        group_norm = take_group(log_norm)
        group_cotangent = take_group(cotangent)

        def owner_step(owner):
            chosen = jnp.nonzero(flat_owner == owner, size=reach, fill_value=entries)[0].astype(jnp.int32)
            valid = chosen < entries
            safe_index = jnp.minimum(chosen, entries - 1)
            token_of = safe_index // VIS
            is_first = (safe_index % VIS) == 0
            token_rows = jnp.where(valid[:, None], group_hidden[token_of], 0).astype(jnp.bfloat16)
            columns = lax.dynamic_slice_in_dim(output_weight, owner * owner_words, owner_words, 1)
            scores = jnp.dot(token_rows, columns, preferred_element_type=jnp.float32)
            picked_negative = group_negative[safe_index]
            picked_mask = group_mask[safe_index]
            target_here = jnp.where(is_first, group_block[token_of], -1)
            matched = (picked_negative[:, :, None] == cluster_ids[None, None, :]) & (picked_mask[:, :, None] == 1)
            cluster_counts = jnp.sum(jnp.where(matched, 1.0, 0.0), axis=1) + jnp.where(target_here[:, None] == cluster_ids[None, :], 1.0, 0.0)
            word_counts = jnp.repeat(cluster_counts, BLOCK, axis=1)
            target_col = (target_here * BLOCK + group_word[token_of]).astype(jnp.float32)
            token_weight = jnp.where(valid, group_cotangent[token_of].astype(jnp.float32), 0.0)
            log_total = group_norm[token_of].astype(jnp.float32)
            target_hot = jnp.where(word_position[None, :] == target_col[:, None], 1.0, 0.0)
            score_grad = (token_weight[:, None] * (word_counts * jnp.exp(scores - log_total[:, None]) - target_hot)).astype(jnp.bfloat16)
            grad_rows = jnp.dot(score_grad, columns.T, preferred_element_type=jnp.float32).astype(jnp.bfloat16)
            weight_part = jnp.dot(token_rows.T, score_grad, preferred_element_type=jnp.float32).astype(jnp.bfloat16)
            return grad_rows, chosen, weight_part

        grad_rows, chosen, weight_part = lax.map(owner_step, jnp.arange(N_VOCAB).astype(jnp.int32))
        per_entry = jnp.zeros((entries, H), jnp.float32).at[chosen.reshape(-1)].set(grad_rows.reshape(-1, H).astype(jnp.float32), mode="drop")
        hidden_group = jnp.sum(per_entry.reshape(GROUP_TOK, VIS, H), axis=1).astype(jnp.bfloat16)
        weight_acc = weight_acc + jnp.moveaxis(weight_part, 0, 1).reshape(H, N_VOCAB * owner_words).astype(jnp.float32)
        return weight_acc, hidden_group

    weight_acc, hidden_parts = lax.scan(group_step, jnp.zeros((H, WORDS), jnp.float32), jnp.arange(N_DP).astype(jnp.int32))
    return hidden_parts.reshape(TOKENS, H), weight_acc.astype(jnp.bfloat16)
```

```python
import jax
import jax.numpy as jnp
from jax import lax
from jax.sharding import PartitionSpec as P

BLOCK = 128
BLK_DEV = 8
META = 128


def body(
    hidden,
    output_weight,
    owners,
    negatives,
    negative_mask,
    target_block,
    target_word,
    log_norm,
    cotangent,
):
    tokens, width = hidden.shape
    visits = owners.shape[1]
    peers = lax.axis_size("vocab")
    words = output_weight.shape[1]
    capacity = max(2, tokens * visits * 4 // (3 * peers))
    slots = peers * capacity
    entries = visits * tokens

    owner = owners.T.reshape(entries)
    owner_hot = owner[:, None] == jnp.arange(peers, dtype=jnp.int32)[None, :]
    entry = jnp.arange(entries, dtype=jnp.int32)
    before = (entry[None, :] < entry[:, None]).astype(jnp.bfloat16)
    earlier = jnp.dot(before, owner_hot.astype(jnp.bfloat16), preferred_element_type=jnp.float32)
    position = jnp.sum(jnp.where(owner_hot, earlier, 0.0), axis=1).astype(jnp.int32)
    slot = owner * capacity + position
    slot_ids = jnp.arange(slots, dtype=jnp.int32)
    place = (slot_ids[:, None] == slot[None, :]).astype(jnp.bfloat16)
    place_token = sum(place[:, v * tokens : (v + 1) * tokens] for v in range(visits))

    cluster = jnp.arange(BLK_DEV, dtype=jnp.int32)
    counts = jnp.sum(
        jnp.where((negatives[..., None] == cluster) & (negative_mask[..., None] == 1), 1.0, 0.0), axis=2
    )
    target_hot = jnp.where(target_block[:, None] == cluster[None, :], 1.0, 0.0)
    counts = counts.at[:, 0].add(target_hot)
    counts = counts.transpose(1, 0, 2).reshape(entries, BLK_DEV)
    first = entry < tokens
    block_here = jnp.where(first, jnp.tile(target_block, visits), -1)
    scalars = jnp.stack(
        [
            jnp.tile(cotangent, visits).astype(jnp.float32),
            jnp.tile(log_norm, visits).astype(jnp.float32),
            block_here.astype(jnp.float32),
            jnp.tile(target_word, visits).astype(jnp.float32),
        ],
        axis=1,
    )
    meta = jnp.concatenate([counts, scalars], axis=1).astype(jnp.bfloat16)
    meta = jnp.pad(meta, ((0, 0), (0, META - meta.shape[1])))

    send = jnp.concatenate(
        [
            jnp.dot(place_token, hidden, preferred_element_type=jnp.float32).astype(jnp.bfloat16),
            jnp.dot(place, meta, preferred_element_type=jnp.float32).astype(jnp.bfloat16),
        ],
        axis=1,
    ).reshape(peers, capacity, width + META)
    got = lax.all_to_all(send, "vocab", split_axis=0, concat_axis=0, tiled=True)
    got = got.reshape(slots, width + META)
    rows = got[:, :width]
    info = got[:, width:].astype(jnp.float32)

    scores = jnp.dot(rows, output_weight, preferred_element_type=jnp.float32)
    word_counts = jnp.broadcast_to(info[:, :BLK_DEV, None], (slots, BLK_DEV, BLOCK)).reshape(slots, words)
    token_weight = info[:, BLK_DEV]
    log_total = info[:, BLK_DEV + 1]
    target_col = info[:, BLK_DEV + 2] * BLOCK + info[:, BLK_DEV + 3]
    word_position = jnp.arange(words).astype(jnp.float32)
    hit = jnp.where(word_position[None, :] == target_col[:, None], 1.0, 0.0)
    score_grad = (
        token_weight[:, None]
        * (jnp.where(word_counts > 0, word_counts * jnp.exp(scores - log_total[:, None]), 0.0) - hit)
    ).astype(jnp.bfloat16)
    weight_part = lax.dot_general(
        rows, score_grad, (((0,), (0,)), ((), ())), preferred_element_type=jnp.float32
    ).astype(jnp.bfloat16)
    weight_grad = lax.psum_scatter(weight_part, "dp", scatter_dimension=0, tiled=True)
    part = lax.dot_general(
        score_grad, output_weight, (((1,), (1,)), ((), ())), preferred_element_type=jnp.float32
    ).astype(jnp.bfloat16)
    back = lax.all_to_all(
        part.reshape(peers, capacity, width), "vocab", split_axis=0, concat_axis=0, tiled=True
    ).reshape(slots, width)
    hidden_grad = lax.dot_general(
        place_token, back, (((0,), (0,)), ((), ())), preferred_element_type=jnp.float32
    ).astype(jnp.bfloat16)
    return (hidden_grad, weight_grad)


def solution(mesh):
    placed = (
        P(("dp", "vocab"), None),
        P(None, "vocab"),
        P(("dp", "vocab"), None),
        P(("dp", "vocab"), None, None),
        P(("dp", "vocab"), None, None),
        P(("dp", "vocab")),
        P(("dp", "vocab")),
        P(("dp", "vocab")),
        P(("dp", "vocab")),
    )
    return jax.shard_map(
        body,
        mesh=mesh,
        in_specs=placed,
        out_specs=(P(("dp", "vocab"), None), P("dp", "vocab")),
        check_vma=False,
    )
```

```python
import functools

import jax
import jax.numpy as jnp
from jax import lax
from jax.experimental import pallas as pl
from jax.experimental.pallas import tpu as pltpu
from jax.sharding import PartitionSpec as P

BLOCK = 128
BLK_DEV = 8
META = 128
GAP = 2
NEAR, STATE, ADD, SUM = 0, 0, 0, 0
MIB = 1 << 20
F32 = jnp.float32
BF16 = jnp.bfloat16
CONTRACT_ROWS = (((0,), (0,)), ((), ()))
CONTRACT_COLS = (((1,), (1,)), ((), ()))


def cost(us):
    return pl.CostEstimate(flops=0, bytes_accessed=int(us * 3.69e6), transcendentals=0)


def params(mib):
    return pltpu.CompilerParams(vmem_limit_bytes=mib * MIB)


def place_kernel(
    capacity,
    hidden_ref,
    owners_ref,
    negatives_ref,
    mask_ref,
    block_ref,
    word_ref,
    norm_ref,
    cot_ref,
    send_ref,
    place_ref,
    send,
    sems,
):
    tokens, width = hidden_ref.shape
    visits, picks = negatives_ref.shape[:2]
    slots = send_ref.shape[0]
    peers = slots // capacity
    owner_iota = lax.broadcasted_iota(jnp.int32, (peers, tokens), 0)
    row = lax.broadcasted_iota(jnp.int32, (tokens, tokens), 0)
    col = lax.broadcasted_iota(jnp.int32, (tokens, tokens), 1)
    before = jnp.where(row < col, 1.0, 0.0).astype(BF16)
    slot_iota = lax.broadcasted_iota(jnp.int32, (slots, tokens), 0)
    cluster = lax.broadcasted_iota(jnp.int32, (BLK_DEV, tokens), 0)
    carried = jnp.zeros((peers, 1), F32)
    block = block_ref[...]
    total = jnp.zeros((slots, tokens), F32)
    info = jnp.zeros((slots, META), F32)
    for v in range(visits):
        owner = owners_ref[v : v + 1, :]
        hot = jnp.where(owner_iota == owner, 1.0, 0.0)
        earlier = jnp.dot(hot.astype(BF16), before, preferred_element_type=F32) + carried
        carried = carried + jnp.sum(hot, axis=1, keepdims=True)
        position = jnp.sum(hot * earlier, axis=0, keepdims=True).astype(jnp.int32)
        place = jnp.where(slot_iota == owner * capacity + position, 1.0, 0.0)
        total = total + place
        counts = jnp.zeros((BLK_DEV, tokens), F32)
        for n in range(picks):
            used = mask_ref[v, n : n + 1, :] == 1
            counts += jnp.where((cluster == negatives_ref[v, n : n + 1, :]) & used, 1.0, 0.0)
        if v == 0:
            counts += jnp.where(cluster == block, 1.0, 0.0)
            here = block.astype(F32)
        else:
            here = jnp.full((1, tokens), -1.0, F32)
        tail = jnp.zeros((META - BLK_DEV - 4, tokens), F32)
        meta = jnp.concatenate(
            [
                counts,
                cot_ref[...].astype(F32),
                norm_ref[...].astype(F32),
                here,
                word_ref[...].astype(F32),
                tail,
            ],
            axis=0,
        ).astype(BF16)
        info += lax.dot_general(
            place.astype(BF16), meta, CONTRACT_COLS, preferred_element_type=F32
        )
    place_tokens = total.astype(BF16)
    place_ref[...] = place_tokens
    send[:, width:] = info.astype(BF16)
    step = 512
    stores = []
    for k, c in enumerate(range(0, width, step)):
        send[:, c : c + step] = jnp.dot(
            place_tokens, hidden_ref[:, c : c + step], preferred_element_type=F32
        ).astype(BF16)
        cut = pl.ds(c, step + META if c + step == width else step)
        stores.append(pltpu.make_async_copy(send.at[:, cut], send_ref.at[:, cut], sems.at[k]))
        stores[-1].start()
    for store in stores:
        store.wait()


def score_kernel(
    chunks_ref, got_ref, weight_ref, grad_ref, up_ref, down_ref, token_ref, rows, weight, meta, acc, sems
):
    steps, _, depth = rows.shape
    loads = []
    for k in range(steps):
        cut = pl.ds(k * depth, depth)
        loads.append(
            (
                pltpu.make_async_copy(got_ref.at[:, cut], rows.at[k], sems.at[0, k]),
                pltpu.make_async_copy(weight_ref.at[cut, :], weight.at[k], sems.at[1, k]),
            )
        )
    last = pltpu.make_async_copy(got_ref.at[:, pl.ds(steps * depth, META)], meta, sems.at[2, 0])
    for pair in loads:
        for load in pair:
            load.start()
    last.start()
    for k, pair in enumerate(loads):
        for load in pair:
            load.wait()
        part = jnp.dot(rows[k], weight[k], preferred_element_type=F32)
        if k == 0:
            acc[...] = part
        else:
            acc[...] += part
    last.wait()
    info = meta[...].astype(F32)
    lane = lax.broadcasted_iota(jnp.int32, (1, BLOCK), 1).astype(F32)
    scale = info[:, BLK_DEV : BLK_DEV + 1]
    norm = info[:, BLK_DEV + 1 : BLK_DEV + 2]
    target = info[:, BLK_DEV + 2 : BLK_DEV + 3] * BLOCK + info[:, BLK_DEV + 3 : BLK_DEV + 4]
    for b in range(BLK_DEV):
        count = info[:, b : b + 1]
        words = slice(b * BLOCK, (b + 1) * BLOCK)
        soft = jnp.where(count > 0, count * jnp.exp(acc[:, words] - norm), 0.0)
        hit = jnp.where(lane + (b * BLOCK) == target, 1.0, 0.0)
        grad_ref[:, words] = (scale * (soft - hit)).astype(BF16)
    half = up_ref.shape[1]
    first = lax.dot_general(
        rows[chunks_ref[steps // 2]], grad_ref[...], CONTRACT_ROWS, preferred_element_type=F32
    )
    up_ref[...] = first[:, :half].astype(BF16)
    down_ref[...] = first[:, half:].astype(BF16)
    token_ref[...] = jnp.zeros_like(token_ref)


def pair_kernel(chunks_ref, rows_up_ref, rows_down_ref, grad_ref, up_ref, down_ref):
    half = up_ref.shape[1]
    up_ref[...] = lax.dot_general(
        rows_up_ref[...], grad_ref[:, half:], CONTRACT_ROWS, preferred_element_type=F32
    ).astype(BF16)
    down_ref[...] = lax.dot_general(
        rows_down_ref[...], grad_ref[:, :half], CONTRACT_ROWS, preferred_element_type=F32
    ).astype(BF16)


def back_kernel(grad_ref, weight_ref, after_ref, part_ref, token_ref, weight, part, sems):
    steps, depth, _ = weight.shape
    loads = [
        pltpu.make_async_copy(weight_ref.at[pl.ds(k * depth, depth), :], weight.at[k], sems.at[0, k])
        for k in range(steps)
    ]
    stores = [
        pltpu.make_async_copy(part.at[k], part_ref.at[:, pl.ds(k * depth, depth)], sems.at[1, k])
        for k in range(steps)
    ]
    for load in loads:
        load.start()
    for k in range(steps):
        loads[k].wait()
        part[k] = lax.dot_general(
            grad_ref[...], weight[k], CONTRACT_COLS, preferred_element_type=F32
        ).astype(BF16)
        stores[k].start()
    for store in stores:
        store.wait()
    token_ref[...] = jnp.zeros_like(token_ref)


def add_kernel(chunks_ref, got_ref, rows_ref, grad_ref, after_ref, out_ref, token_ref):
    out_ref[...] = (
        got_ref[...].astype(F32)
        + lax.dot_general(rows_ref[...], grad_ref[...], CONTRACT_ROWS, preferred_element_type=F32)
    ).astype(BF16)
    token_ref[...] = jnp.zeros_like(token_ref)


def last_kernel(
    chunks_ref, low_up_ref, low_down_ref, high_up_ref, high_down_ref, rows_ref, grad_ref, after_ref, out_ref
):
    half = low_up_ref.shape[1]
    own = lax.dot_general(rows_ref[...], grad_ref[...], CONTRACT_ROWS, preferred_element_type=F32)
    low = low_up_ref[...].astype(F32) + low_down_ref[...].astype(F32)
    high = high_up_ref[...].astype(F32) + high_down_ref[...].astype(F32)
    out_ref[:, :half] = (own[:, :half] + low).astype(BF16)
    out_ref[:, half:] = (own[:, half:] + high).astype(BF16)


def sum_kernel(place_ref, back_ref, after_ref, out_ref, token_ref):
    out_ref[...] = lax.dot_general(
        place_ref[...], back_ref[...], CONTRACT_ROWS, preferred_element_type=F32
    ).astype(BF16)
    token_ref[...] = jnp.zeros_like(token_ref)


def body(
    hidden,
    output_weight,
    owners,
    negatives,
    negative_mask,
    target_block,
    target_word,
    log_norm,
    cotangent,
):
    tokens, width = hidden.shape
    visits = owners.shape[1]
    peers = lax.axis_size("vocab")
    planes = lax.axis_size("dp")
    words = output_weight.shape[1]
    capacity = max(2, tokens * visits * 4 // (3 * peers))
    slots = peers * capacity
    sent = width + META
    chunk = width // planes
    half = words // 2
    weights = pltpu.with_memory_space_constraint(output_weight, pltpu.HBM)
    anywhere = pl.BlockSpec(memory_space=pl.ANY)
    hbm = pl.BlockSpec(memory_space=pltpu.HBM)
    vmem = pl.BlockSpec(memory_space=pltpu.VMEM)
    steps = 8
    depth = width // steps

    send, place = pl.pallas_call(
        functools.partial(place_kernel, capacity),
        in_specs=[vmem] * 8,
        out_specs=[hbm, vmem],
        out_shape=[
            pltpu.HBM((slots, sent), BF16),
            jax.ShapeDtypeStruct((slots, tokens), BF16),
        ],
        scratch_shapes=[pltpu.VMEM((slots, sent), BF16), pltpu.SemaphoreType.DMA((width // 512,))],
        compiler_params=params(24),
        cost_estimate=cost(0),
        name="place_rows",
    )(
        hidden,
        owners.T,
        negatives.transpose(1, 2, 0),
        negative_mask.transpose(1, 2, 0),
        target_block[None, :],
        target_word[None, :],
        log_norm[None, :],
        cotangent[None, :],
    )
    got = lax.all_to_all(
        send.reshape(peers, capacity, sent), "vocab", split_axis=0, concat_axis=0, tiled=True
    ).reshape(slots, sent)

    chunks = lax.rem(lax.axis_index("dp") + jnp.arange(planes, dtype=jnp.int32), planes)
    far = planes // 2

    def rows_spec(k):
        return pl.BlockSpec((slots, chunk), lambda i, c: (0, c[k % planes]))

    def whole(shape):
        return pl.BlockSpec(shape, lambda i, c: (0, 0))

    message = jax.ShapeDtypeStruct((chunk, half), BF16)
    message_spec = whole((chunk, half))
    token = jax.ShapeDtypeStruct((8, 128), F32)
    token_spec = whole((8, 128))
    grad, far_up, far_down, _ = pl.pallas_call(
        score_kernel,
        grid_spec=pltpu.PrefetchScalarGridSpec(
            num_scalar_prefetch=1,
            grid=(1,),
            in_specs=[hbm, hbm],
            out_specs=[whole((slots, words)), message_spec, message_spec, token_spec],
            scratch_shapes=[
                pltpu.VMEM((steps, slots, depth), BF16),
                pltpu.VMEM((steps, depth, words), BF16),
                pltpu.VMEM((slots, META), BF16),
                pltpu.VMEM((slots, words), F32),
                pltpu.SemaphoreType.DMA((3, steps)),
            ],
        ),
        out_shape=[jax.ShapeDtypeStruct((slots, words), BF16), message, message, token],
        compiler_params=params(32),
        cost_estimate=cost(0),
        name="scores",
    )(chunks, got, weights)

    def hop(x, d):
        return lax.ppermute(x, "dp", [(i, (i + d) % planes) for i in range(planes)])

    near = far - 1
    near_up, near_down = pl.pallas_call(
        pair_kernel,
        grid_spec=pltpu.PrefetchScalarGridSpec(
            num_scalar_prefetch=1,
            grid=(1,),
            in_specs=[rows_spec(near), rows_spec(-near), whole((slots, words))],
            out_specs=[message_spec, message_spec],
        ),
        out_shape=[message, message],
        compiler_params=params(16),
        cost_estimate=cost(NEAR),
        name="near_parts",
    )(chunks, got, got, grad)

    def state_parts(after):
        return pl.pallas_call(
            back_kernel,
            in_specs=[vmem, hbm, anywhere],
            out_specs=[hbm, vmem],
            out_shape=[pltpu.HBM((slots, width), BF16), token],
            scratch_shapes=[
                pltpu.VMEM((steps, depth, words), BF16),
                pltpu.VMEM((steps, slots, depth), BF16),
                pltpu.SemaphoreType.DMA((2, steps)),
            ],
            compiler_params=params(24),
            cost_estimate=cost(STATE),
            name="state_parts",
        )(grad, weights, after)

    def add(k, high, arrived, after):
        return pl.pallas_call(
            add_kernel,
            grid_spec=pltpu.PrefetchScalarGridSpec(
                num_scalar_prefetch=1,
                grid=(1,),
                in_specs=[
                    message_spec,
                    rows_spec(k),
                    pl.BlockSpec((slots, half), lambda i, c: (0, high)),
                    anywhere,
                ],
                out_specs=[message_spec, token_spec],
            ),
            out_shape=[message, token],
            compiler_params=params(16),
            cost_estimate=cost(ADD),
            name="add_part",
        )(chunks, arrived, got, grad, after)

    flows = [(1, 0, far, far_up), (-1, 1, far, far_down), (1, 1, near, near_up), (-1, 0, near, near_down)]
    messages = [f[3] for f in flows]
    after = near_up
    event = 0
    for step in range(far):
        for f, (d, high, hops, _) in enumerate(flows):
            if step < hops:
                messages[f] = hop(messages[f], d)
                if step < hops - 1:
                    messages[f], after = add(d * (hops - 1 - step), high, messages[f], after)
                    event += 1
                    if event == GAP:
                        part, after = state_parts(after)
    back = lax.all_to_all(
        part.reshape(peers, capacity, width), "vocab", split_axis=0, concat_axis=0, tiled=True
    ).reshape(slots, width)

    hidden_grad, after = pl.pallas_call(
        sum_kernel,
        grid=(4,),
        in_specs=[
            pl.BlockSpec((slots, tokens), lambda i: (0, 0)),
            pl.BlockSpec((slots, width // 4), lambda i: (0, i)),
            anywhere,
        ],
        out_specs=[
            pl.BlockSpec((tokens, width // 4), lambda i: (0, i)),
            pl.BlockSpec((8, 128), lambda i: (0, 0)),
        ],
        out_shape=[jax.ShapeDtypeStruct((tokens, width), BF16), token],
        compiler_params=params(16),
        cost_estimate=cost(SUM),
        name="sum_parts",
    )(place, back, after)

    weight_grad = pl.pallas_call(
        last_kernel,
        grid_spec=pltpu.PrefetchScalarGridSpec(
            num_scalar_prefetch=1,
            grid=(1,),
            in_specs=[message_spec] * 4 + [rows_spec(0), whole((slots, words)), anywhere],
            out_specs=whole((chunk, words)),
        ),
        out_shape=jax.ShapeDtypeStruct((chunk, words), BF16),
        compiler_params=params(24),
        cost_estimate=cost(0),
        name="last_add",
    )(chunks, messages[0], messages[3], messages[1], messages[2], got, grad, after)
    return (hidden_grad, weight_grad)


def solution(mesh):
    placed = (
        P(("dp", "vocab"), None),
        P(None, "vocab"),
        P(("dp", "vocab"), None),
        P(("dp", "vocab"), None, None),
        P(("dp", "vocab"), None, None),
        P(("dp", "vocab")),
        P(("dp", "vocab")),
        P(("dp", "vocab")),
        P(("dp", "vocab")),
    )
    return jax.shard_map(
        body,
        mesh=mesh,
        in_specs=placed,
        out_specs=(P(("dp", "vocab"), None), P("dp", "vocab")),
        check_vma=False,
    )
```

```python
import functools

import jax
import jax.numpy as jnp
from jax import lax
from jax.experimental import pallas as pl
from jax.experimental.pallas import tpu as pltpu
from jax.sharding import PartitionSpec as P

BLOCK = 128
BLK_DEV = 8
META = 128
GAP = 0
STEPS = 4
MIB = 1 << 20
F32 = jnp.float32
BF16 = jnp.bfloat16
HOPS_US = (3,) * 10
OWN_US, SUM_US, LATE_US = 100, 0, 0


def cost(us):
    return pl.CostEstimate(flops=int(us * 1.15e9), bytes_accessed=0, transcendentals=0)


CONTRACT_ROWS = (((0,), (0,)), ((), ()))
CONTRACT_COLS = (((1,), (1,)), ((), ()))


def params(mib):
    return pltpu.CompilerParams(vmem_limit_bytes=mib * MIB)


def place_kernel(
    capacity,
    hidden_ref,
    owners_ref,
    negatives_ref,
    mask_ref,
    block_ref,
    word_ref,
    norm_ref,
    cot_ref,
    send_ref,
    place_ref,
    hidden,
    send,
    sems,
):
    tokens, width = hidden_ref.shape
    load = pltpu.make_async_copy(hidden_ref, hidden, sems.at[width // 512])
    load.start()
    visits, picks = negatives_ref.shape[:2]
    slots = send_ref.shape[0]
    peers = slots // capacity
    owner_iota = lax.broadcasted_iota(jnp.int32, (peers, tokens), 0)
    row = lax.broadcasted_iota(jnp.int32, (tokens, tokens), 0)
    col = lax.broadcasted_iota(jnp.int32, (tokens, tokens), 1)
    before = jnp.where(row < col, 1.0, 0.0).astype(BF16)
    slot_iota = lax.broadcasted_iota(jnp.int32, (slots, tokens), 0)
    cluster = lax.broadcasted_iota(jnp.int32, (BLK_DEV, tokens), 0)
    carried = jnp.zeros((peers, 1), F32)
    block = block_ref[...]
    total = jnp.zeros((slots, tokens), F32)
    info = jnp.zeros((slots, META), F32)
    for v in range(visits):
        owner = owners_ref[v : v + 1, :]
        hot = jnp.where(owner_iota == owner, 1.0, 0.0)
        earlier = jnp.dot(hot.astype(BF16), before, preferred_element_type=F32) + carried
        carried = carried + jnp.sum(hot, axis=1, keepdims=True)
        position = jnp.sum(hot * earlier, axis=0, keepdims=True).astype(jnp.int32)
        place = jnp.where(slot_iota == owner * capacity + position, 1.0, 0.0)
        total = total + place
        counts = jnp.zeros((BLK_DEV, tokens), F32)
        for n in range(picks):
            used = mask_ref[v, n : n + 1, :] == 1
            counts += jnp.where((cluster == negatives_ref[v, n : n + 1, :]) & used, 1.0, 0.0)
        if v == 0:
            counts += jnp.where(cluster == block, 1.0, 0.0)
            here = block.astype(F32)
        else:
            here = jnp.full((1, tokens), -1.0, F32)
        tail = jnp.zeros((META - BLK_DEV - 4, tokens), F32)
        meta = jnp.concatenate(
            [
                counts,
                cot_ref[...].astype(F32),
                norm_ref[...].astype(F32),
                here,
                word_ref[...].astype(F32),
                tail,
            ],
            axis=0,
        ).astype(BF16)
        info += lax.dot_general(
            place.astype(BF16), meta, CONTRACT_COLS, preferred_element_type=F32
        )
    place_tokens = total.astype(BF16)
    place_ref[...] = place_tokens
    send[:, width:] = info.astype(BF16)
    step = 512
    load.wait()
    stores = []
    for k, c in enumerate(range(0, width, step)):
        send[:, c : c + step] = jnp.dot(
            place_tokens, hidden[:, c : c + step], preferred_element_type=F32
        ).astype(BF16)
        cut = pl.ds(c, step + META if c + step == width else step)
        stores.append(pltpu.make_async_copy(send.at[:, cut], send_ref.at[:, cut], sems.at[k]))
        stores[-1].start()
    for store in stores:
        store.wait()


def turn_kernel(place_ref, placed_ref):
    placed_ref[...] = place_ref[...].astype(F32).T.astype(BF16)


def score_half(high, chunks_ref, rows_ref, meta_ref, weight, grad_ref, far_ref, near_ref, acc, ready):
    steps, depth, half = weight.shape
    base = high * half
    for k in range(steps):
        ready(k)
        part = jnp.dot(
            rows_ref[:, k * depth : (k + 1) * depth], weight[k], preferred_element_type=F32
        )
        if k == 0:
            acc[...] = part
        else:
            acc[...] += part
    ready(steps)
    info = meta_ref[...].astype(F32)
    lane = lax.broadcasted_iota(jnp.int32, (1, BLOCK), 1).astype(F32)
    scale = info[:, BLK_DEV : BLK_DEV + 1]
    norm = info[:, BLK_DEV + 1 : BLK_DEV + 2]
    target = info[:, BLK_DEV + 2 : BLK_DEV + 3] * BLOCK + info[:, BLK_DEV + 3 : BLK_DEV + 4]
    for b in range(half // BLOCK):
        first = base + b * BLOCK
        count = info[:, first // BLOCK : first // BLOCK + 1]
        words = slice(b * BLOCK, (b + 1) * BLOCK)
        soft = jnp.where(count > 0, count * jnp.exp(acc[:, words] - norm), 0.0)
        hit = jnp.where(lane + first == target, 1.0, 0.0)
        grad_ref[:, words] = (scale * (soft - hit)).astype(BF16)
    chunk = far_ref.shape[0]
    far = rows_ref.shape[1] // chunk // 2
    near = far - 1 if high else far + 1
    for k, out_ref in ((far, far_ref), (near, near_ref)):
        out_ref[...] = lax.dot_general(
            rows_ref[:, pl.ds(pl.multiple_of(chunks_ref[k] * chunk, chunk), chunk)],
            grad_ref[...],
            CONTRACT_ROWS,
            preferred_element_type=F32,
        ).astype(BF16)


def weight_loads(weight_ref, weight, sems, base):
    steps, depth, half = weight.shape
    return [
        pltpu.make_async_copy(
            weight_ref.at[pl.ds(k * depth, depth), pl.ds(base, half)], weight.at[k], sems.at[0, k]
        )
        for k in range(steps)
    ]


def low_kernel(
    chunks_ref, got_ref, weight_ref, after_ref, rows_ref, meta_ref, grad_ref, far_ref, near_ref, weight, acc, sems
):
    steps, depth, _ = weight.shape
    weights = weight_loads(weight_ref, weight, sems, 0)
    loads = []
    for k in range(steps):
        cut = pl.ds(k * depth, depth)
        loads.append(pltpu.make_async_copy(got_ref.at[:, cut], rows_ref.at[:, cut], sems.at[1, k]))
    last = pltpu.make_async_copy(got_ref.at[:, pl.ds(steps * depth, META)], meta_ref, sems.at[0, steps])
    for k in range(steps):
        weights[k].start()
        loads[k].start()
    last.start()

    def ready(k):
        if k == steps:
            last.wait()
        else:
            weights[k].wait()
            loads[k].wait()

    score_half(0, chunks_ref, rows_ref, meta_ref, weight, grad_ref, far_ref, near_ref, acc, ready)


def high_kernel(
    chunks_ref, rows_ref, meta_ref, weight_ref, grad_ref, far_ref, near_ref, weight, acc, sems
):
    loads = weight_loads(weight_ref, weight, sems, weight.shape[2])
    for load in loads:
        load.start()

    def ready(k):
        if k < len(loads):
            loads[k].wait()

    score_half(1, chunks_ref, rows_ref, meta_ref, weight, grad_ref, far_ref, near_ref, acc, ready)


def back_kernel(low_ref, high_ref, weight_ref, after_ref, part_ref, token_ref, grad, weight, part, sems):
    steps, depth, _ = weight.shape
    half = low_ref.shape[1]
    loads = [
        pltpu.make_async_copy(weight_ref.at[pl.ds(k * depth, depth), :], weight.at[k], sems.at[0, k])
        for k in range(steps)
    ]
    stores = [
        pltpu.make_async_copy(part.at[k], part_ref.at[:, pl.ds(k * depth, depth)], sems.at[1, k])
        for k in range(steps)
    ]
    for load in loads:
        load.start()
    grad[:, :half] = low_ref[...]
    grad[:, half:] = high_ref[...]
    for k in range(steps):
        loads[k].wait()
        part[k] = lax.dot_general(
            grad[...], weight[k], CONTRACT_COLS, preferred_element_type=F32
        ).astype(BF16)
        stores[k].start()
    for store in stores:
        store.wait()
    token_ref[...] = jnp.zeros_like(token_ref)


def add_kernel(chunks_ref, got_ref, rows_ref, grad_ref, after_ref, out_ref, token_ref):
    own = lax.dot_general(rows_ref[...], grad_ref[...], CONTRACT_ROWS, preferred_element_type=F32)
    out_ref[...] = (got_ref[...].astype(F32) + own).astype(BF16)
    token_ref[...] = jnp.zeros_like(token_ref)


def own_kernel(chunks_ref, low_near_ref, high_near_ref, rows_ref, low_ref, high_ref, after_ref, out_ref, token_ref):
    half = low_ref.shape[1]
    token_ref[...] = jnp.zeros_like(token_ref)
    for k, near_ref, grad_ref in ((0, low_near_ref, low_ref), (1, high_near_ref, high_ref)):
        own = lax.dot_general(rows_ref[...], grad_ref[...], CONTRACT_ROWS, preferred_element_type=F32)
        out_ref[:, k * half : (k + 1) * half] = near_ref[...].astype(F32) + own


def last_kernel(low_far_ref, high_far_ref, own_ref, after_ref, out_ref):
    half = low_far_ref.shape[1]
    for k, far_ref in enumerate((low_far_ref, high_far_ref)):
        cut = slice(k * half, (k + 1) * half)
        out_ref[:, cut] = (own_ref[:, cut] + far_ref[...].astype(F32)).astype(BF16)


def sum_kernel(placed_ref, back_ref, after_ref, out_ref, token_ref):
    out_ref[...] = jnp.dot(placed_ref[...], back_ref[...], preferred_element_type=F32).astype(BF16)
    token_ref[...] = jnp.zeros_like(token_ref)


def body(
    hidden,
    output_weight,
    owners,
    negatives,
    negative_mask,
    target_block,
    target_word,
    log_norm,
    cotangent,
):
    tokens, width = hidden.shape
    visits = owners.shape[1]
    peers = lax.axis_size("vocab")
    planes = lax.axis_size("dp")
    words = output_weight.shape[1]
    capacity = max(2, tokens * visits * 4 // (3 * peers))
    slots = peers * capacity
    sent = width + META
    chunk = width // planes
    half = words // 2
    def in_hbm(x):
        return pltpu.with_memory_space_constraint(x, pltpu.HBM)

    anywhere = pl.BlockSpec(memory_space=pl.ANY)
    hbm = pl.BlockSpec(memory_space=pltpu.HBM)
    vmem = pl.BlockSpec(memory_space=pltpu.VMEM)
    smem = pl.BlockSpec(memory_space=pltpu.SMEM)
    far = planes // 2
    near = far - 1

    def whole(*shape):
        return pl.BlockSpec(shape, lambda i: (0,) * len(shape))

    smalls = [
        owners.T,
        negatives.transpose(1, 2, 0),
        negative_mask.transpose(1, 2, 0),
        target_block[None, :],
        target_word[None, :],
        log_norm[None, :],
        cotangent[None, :],
    ]
    send, place = pl.pallas_call(
        functools.partial(place_kernel, capacity),
        grid=(1,),
        in_specs=[hbm] + [whole(*x.shape) for x in smalls],
        out_specs=[hbm, whole(slots, tokens)],
        out_shape=[
            pltpu.HBM((slots, sent), BF16),
            jax.ShapeDtypeStruct((slots, tokens), BF16),
        ],
        scratch_shapes=[
            pltpu.VMEM((tokens, width), BF16),
            pltpu.VMEM((slots, sent), BF16),
            pltpu.SemaphoreType.DMA((width // 512 + 1,)),
        ],
        compiler_params=params(24),
        cost_estimate=cost(0),
        name="place_rows",
    )(*[in_hbm(x) for x in (hidden, *smalls)])
    got = lax.all_to_all(
        send.reshape(peers, capacity, sent), "vocab", split_axis=0, concat_axis=0, tiled=True
    ).reshape(slots, sent)

    placed = pl.pallas_call(
        turn_kernel,
        in_specs=[vmem],
        out_specs=vmem,
        out_shape=jax.ShapeDtypeStruct((tokens, slots), BF16),
        cost_estimate=cost(100),
        compiler_params=params(4),
        name="turn_places",
    )(place)
    weights = in_hbm(output_weight)
    got = in_hbm(got)
    chunks = lax.rem(lax.axis_index("dp") + jnp.arange(planes, dtype=jnp.int32), planes)

    message = jax.ShapeDtypeStruct((chunk, half), BF16)
    grad_half = jax.ShapeDtypeStruct((slots, half), BF16)
    token = jax.ShapeDtypeStruct((8, 128), F32)
    acc = pltpu.VMEM((slots, half), F32)
    half_weight = pltpu.VMEM((STEPS, width // STEPS, half), BF16)
    rows, meta, low, low_far, low_near = pl.pallas_call(
        low_kernel,
        in_specs=[smem, hbm, hbm, anywhere],
        out_specs=[vmem] * 5,
        out_shape=[
            jax.ShapeDtypeStruct((slots, width), BF16),
            jax.ShapeDtypeStruct((slots, META), BF16),
            grad_half,
            message,
            message,
        ],
        scratch_shapes=[half_weight, acc, pltpu.SemaphoreType.DMA((2, STEPS + 1))],
        compiler_params=params(20),
        cost_estimate=cost(0),
        name="low_scores",
    )(chunks, got, weights, placed)
    high, high_far, high_near = pl.pallas_call(
        high_kernel,
        in_specs=[smem, vmem, vmem, hbm],
        out_specs=[vmem] * 3,
        out_shape=[grad_half, message, message],
        scratch_shapes=[half_weight, acc, pltpu.SemaphoreType.DMA((1, STEPS))],
        compiler_params=params(20),
        cost_estimate=cost(LATE_US),
        name="high_scores",
    )(chunks, rows, meta, weights)

    def hop(x, d):
        return lax.ppermute(x, "dp", [(i, (i + d) % planes) for i in range(planes)])

    def rows_spec(k):
        return pl.BlockSpec((slots, chunk), lambda i, c: (0, c[k % planes]))

    message_spec = pl.BlockSpec((chunk, half), lambda i, c: (0, 0))
    token_spec = pl.BlockSpec((8, 128), lambda i, c: (0, 0))

    def state_parts(after):
        return pl.pallas_call(
            back_kernel,
            in_specs=[vmem, vmem, hbm, anywhere],
            out_specs=[hbm, vmem],
            out_shape=[pltpu.HBM((slots, width), BF16), token],
            scratch_shapes=[
                pltpu.VMEM((slots, words), BF16),
                pltpu.VMEM((planes, chunk, words), BF16),
                pltpu.VMEM((planes, slots, chunk), BF16),
                pltpu.SemaphoreType.DMA((2, planes)),
            ],
            compiler_params=params(24),
            cost_estimate=cost(LATE_US),
            name="state_parts",
        )(low, high, weights, after)

    def add(k, grad, arrived, after, us):
        return pl.pallas_call(
            add_kernel,
            grid_spec=pltpu.PrefetchScalarGridSpec(
                num_scalar_prefetch=1,
                grid=(1,),
                in_specs=[message_spec, rows_spec(k), message_spec, anywhere],
                out_specs=[message_spec, token_spec],
            ),
            out_shape=[message, token],
            compiler_params=params(12),
            cost_estimate=cost(us),
            name="add_part",
        )(chunks, arrived, got, grad, after)

    flows = [(1, low, far), (-1, low, near), (-1, high, far), (1, high, near)]
    messages = [low_far, low_near, high_far, high_near]
    after = high_near
    event = 0
    for step in range(far):
        for f, (d, grad, hops) in enumerate(flows):
            if step < hops:
                messages[f] = hop(messages[f], d)
                if step < hops - 1:
                    if event == GAP:
                        part, after = state_parts(after)
                    messages[f], after = add(
                        d * (hops - 1 - step), grad, messages[f], after, HOPS_US[event]
                    )
                    event += 1
    back = lax.all_to_all(
        part.reshape(peers, capacity, width), "vocab", split_axis=0, concat_axis=0, tiled=True
    ).reshape(slots, width)

    own, after = pl.pallas_call(
        own_kernel,
        grid_spec=pltpu.PrefetchScalarGridSpec(
            num_scalar_prefetch=1,
            grid=(1,),
            in_specs=[message_spec] * 2 + [rows_spec(0)] + [message_spec] * 2 + [anywhere],
            out_specs=[pl.BlockSpec((chunk, words), lambda i, c: (0, 0)), token_spec],
        ),
        out_shape=[jax.ShapeDtypeStruct((chunk, words), F32), token],
        compiler_params=params(16),
        cost_estimate=cost(OWN_US),
        name="own_part",
    )(chunks, messages[1], messages[3], got, low, high, after)
    pieces = 4
    hidden_grad, after = pl.pallas_call(
        sum_kernel,
        grid=(pieces,),
        in_specs=[
            whole(tokens, slots),
            pl.BlockSpec((slots, width // pieces), lambda i: (0, i)),
            anywhere,
        ],
        out_specs=[pl.BlockSpec((tokens, width // pieces), lambda i: (0, i)), whole(8, 128)],
        out_shape=[jax.ShapeDtypeStruct((tokens, width), BF16), token],
        compiler_params=params(12),
        cost_estimate=cost(SUM_US),
        name="sum_parts",
    )(placed, in_hbm(back), after)

    weight_grad = pl.pallas_call(
        last_kernel,
        in_specs=[vmem, vmem, vmem, anywhere],
        out_specs=vmem,
        out_shape=jax.ShapeDtypeStruct((chunk, words), BF16),
        compiler_params=params(12),
        cost_estimate=cost(0),
        name="last_add",
    )(messages[0], messages[2], own, after)
    return (hidden_grad, weight_grad)


def solution(mesh):
    placed = (
        P(("dp", "vocab"), None),
        P(None, "vocab"),
        P(("dp", "vocab"), None),
        P(("dp", "vocab"), None, None),
        P(("dp", "vocab"), None, None),
        P(("dp", "vocab")),
        P(("dp", "vocab")),
        P(("dp", "vocab")),
        P(("dp", "vocab")),
    )
    return jax.shard_map(
        body,
        mesh=mesh,
        in_specs=placed,
        out_specs=(P(("dp", "vocab"), None), P("dp", "vocab")),
        check_vma=False,
    )
```

```python
import functools

import jax
import jax.numpy as jnp
from jax import lax
from jax.experimental import pallas as pl
from jax.experimental.pallas import tpu as pltpu
from jax.sharding import PartitionSpec as P

BLOCK = 128
BLK_DEV = 8
META = 128
GAP = 0
STEPS = 4
LOW_BLOCKS = 5
MIB = 1 << 20
F32 = jnp.float32
BF16 = jnp.bfloat16
HOPS_US = (3,) * 10
OWN_US, SUM_US, HIGH_US, STATE_US, LAST_US = 100, 0, 0, 0, 0


def cost(us):
    return pl.CostEstimate(flops=int(us * 1.15e9), bytes_accessed=0, transcendentals=0)


CONTRACT_ROWS = (((0,), (0,)), ((), ()))
CONTRACT_COLS = (((1,), (1,)), ((), ()))


def params(mib):
    return pltpu.CompilerParams(vmem_limit_bytes=mib * MIB)


def place_kernel(
    capacity,
    hidden_ref,
    owners_ref,
    negatives_ref,
    mask_ref,
    block_ref,
    word_ref,
    norm_ref,
    cot_ref,
    send_ref,
    place_ref,
    hidden,
    send,
    sems,
):
    tokens, width = hidden_ref.shape
    load = pltpu.make_async_copy(hidden_ref, hidden, sems.at[width // 512])
    load.start()
    visits, picks = negatives_ref.shape[:2]
    slots = send_ref.shape[0]
    peers = slots // capacity
    owner_iota = lax.broadcasted_iota(jnp.int32, (peers, tokens), 0)
    row = lax.broadcasted_iota(jnp.int32, (tokens, tokens), 0)
    col = lax.broadcasted_iota(jnp.int32, (tokens, tokens), 1)
    before = jnp.where(row < col, 1.0, 0.0).astype(BF16)
    slot_iota = lax.broadcasted_iota(jnp.int32, (slots, tokens), 0)
    cluster = lax.broadcasted_iota(jnp.int32, (BLK_DEV, tokens), 0)
    carried = jnp.zeros((peers, 1), F32)
    block = block_ref[...]
    total = jnp.zeros((slots, tokens), F32)
    info = jnp.zeros((slots, META), F32)
    for v in range(visits):
        owner = owners_ref[v : v + 1, :]
        hot = jnp.where(owner_iota == owner, 1.0, 0.0)
        earlier = jnp.dot(hot.astype(BF16), before, preferred_element_type=F32) + carried
        carried = carried + jnp.sum(hot, axis=1, keepdims=True)
        position = jnp.sum(hot * earlier, axis=0, keepdims=True).astype(jnp.int32)
        place = jnp.where(slot_iota == owner * capacity + position, 1.0, 0.0)
        total = total + place
        counts = jnp.zeros((BLK_DEV, tokens), F32)
        for n in range(picks):
            used = mask_ref[v, n : n + 1, :] == 1
            counts += jnp.where((cluster == negatives_ref[v, n : n + 1, :]) & used, 1.0, 0.0)
        if v == 0:
            counts += jnp.where(cluster == block, 1.0, 0.0)
            here = block.astype(F32)
        else:
            here = jnp.full((1, tokens), -1.0, F32)
        tail = jnp.zeros((META - BLK_DEV - 4, tokens), F32)
        meta = jnp.concatenate(
            [
                counts,
                cot_ref[...].astype(F32),
                norm_ref[...].astype(F32),
                here,
                word_ref[...].astype(F32),
                tail,
            ],
            axis=0,
        ).astype(BF16)
        info += lax.dot_general(
            place.astype(BF16), meta, CONTRACT_COLS, preferred_element_type=F32
        )
    place_tokens = total.astype(BF16)
    place_ref[...] = place_tokens
    send[:, width:] = info.astype(BF16)
    step = 512
    load.wait()
    stores = []
    for k, c in enumerate(range(0, width, step)):
        send[:, c : c + step] = jnp.dot(
            place_tokens, hidden[:, c : c + step], preferred_element_type=F32
        ).astype(BF16)
        cut = pl.ds(c, step + META if c + step == width else step)
        stores.append(pltpu.make_async_copy(send.at[:, cut], send_ref.at[:, cut], sems.at[k]))
        stores[-1].start()
    for store in stores:
        store.wait()


def turn_kernel(place_ref, placed_ref):
    placed_ref[...] = place_ref[...].astype(F32).T.astype(BF16)


def score_half(base, chunks_ref, rows_ref, meta_ref, weight, grad_ref, far_ref, near_ref, acc, ready):
    steps, depth, half = weight.shape
    for k in range(steps):
        ready(k)
        part = jnp.dot(
            rows_ref[:, k * depth : (k + 1) * depth], weight[k], preferred_element_type=F32
        )
        if k == 0:
            acc[...] = part
        else:
            acc[...] += part
    ready(steps)
    info = meta_ref[...].astype(F32)
    lane = lax.broadcasted_iota(jnp.int32, (1, BLOCK), 1).astype(F32)
    scale = info[:, BLK_DEV : BLK_DEV + 1]
    norm = info[:, BLK_DEV + 1 : BLK_DEV + 2]
    target = info[:, BLK_DEV + 2 : BLK_DEV + 3] * BLOCK + info[:, BLK_DEV + 3 : BLK_DEV + 4]
    for b in range(half // BLOCK):
        first = base + b * BLOCK
        count = info[:, first // BLOCK : first // BLOCK + 1]
        words = slice(b * BLOCK, (b + 1) * BLOCK)
        soft = jnp.where(count > 0, count * jnp.exp(acc[:, words] - norm), 0.0)
        hit = jnp.where(lane + first == target, 1.0, 0.0)
        grad_ref[:, words] = (scale * (soft - hit)).astype(BF16)
    chunk = far_ref.shape[0]
    far = rows_ref.shape[1] // chunk // 2
    near = far - 1 if base else far + 1
    for k, out_ref in ((far, far_ref), (near, near_ref)):
        out_ref[...] = lax.dot_general(
            rows_ref[:, pl.ds(pl.multiple_of(chunks_ref[k] * chunk, chunk), chunk)],
            grad_ref[...],
            CONTRACT_ROWS,
            preferred_element_type=F32,
        ).astype(BF16)


def weight_loads(weight_ref, weight, sems, base):
    steps, depth, some = weight.shape
    return [
        pltpu.make_async_copy(
            weight_ref.at[pl.ds(k * depth, depth), pl.ds(base, some)], weight.at[k], sems.at[k]
        )
        for k in range(steps)
    ]


def low_kernel(
    chunks_ref,
    got_ref,
    weight_ref,
    after_ref,
    rows_ref,
    meta_ref,
    low_weight,
    high_weight,
    grad_ref,
    far_ref,
    near_ref,
    acc,
    sems,
):
    steps, depth, some = low_weight.shape
    weights = weight_loads(weight_ref, low_weight, sems.at[0], 0)
    others = weight_loads(weight_ref, high_weight, sems.at[1], some)
    loads = []
    for k in range(steps):
        cut = pl.ds(k * depth, depth)
        loads.append(pltpu.make_async_copy(got_ref.at[:, cut], rows_ref.at[:, cut], sems.at[2, k]))
    last = pltpu.make_async_copy(got_ref.at[:, pl.ds(steps * depth, META)], meta_ref, sems.at[3, 0])
    for k in range(steps):
        weights[k].start()
        loads[k].start()
    last.start()
    for other in others:
        other.start()

    def ready(k):
        if k == steps:
            last.wait()
        else:
            weights[k].wait()
            loads[k].wait()

    score_half(0, chunks_ref, rows_ref, meta_ref, low_weight, grad_ref, far_ref, near_ref, acc, ready)
    for other in others:
        other.wait()


def high_kernel(base, chunks_ref, rows_ref, meta_ref, weight, grad_ref, far_ref, near_ref, acc):
    score_half(
        base, chunks_ref, rows_ref, meta_ref, weight, grad_ref, far_ref, near_ref, acc, lambda k: None
    )


def back_kernel(
    low_ref, high_ref, low_weight, high_weight, after_ref, part_ref, token_ref, part, sems
):
    steps, depth, _ = low_weight.shape
    pieces, _, piece = part.shape
    stores = []
    for k in range(pieces):
        step, place = divmod(k * piece, depth)
        cut = slice(place, place + piece)
        total = lax.dot_general(
            low_ref[...], low_weight[step, cut, :], CONTRACT_COLS, preferred_element_type=F32
        ) + lax.dot_general(
            high_ref[...], high_weight[step, cut, :], CONTRACT_COLS, preferred_element_type=F32
        )
        part[k] = total.astype(BF16)
        stores.append(
            pltpu.make_async_copy(part.at[k], part_ref.at[:, pl.ds(k * piece, piece)], sems.at[k])
        )
        stores[k].start()
    for store in stores:
        store.wait()
    token_ref[...] = jnp.zeros_like(token_ref)


def add_kernel(chunks_ref, got_ref, rows_ref, grad_ref, after_ref, out_ref, token_ref):
    own = lax.dot_general(rows_ref[...], grad_ref[...], CONTRACT_ROWS, preferred_element_type=F32)
    out_ref[...] = (got_ref[...].astype(F32) + own).astype(BF16)
    token_ref[...] = jnp.zeros_like(token_ref)


def own_kernel(
    chunks_ref, low_near_ref, high_near_ref, rows_ref, low_ref, high_ref, after_ref, out_ref, token_ref
):
    token_ref[...] = jnp.zeros_like(token_ref)
    base = 0
    for near_ref, grad_ref in ((low_near_ref, low_ref), (high_near_ref, high_ref)):
        own = lax.dot_general(rows_ref[...], grad_ref[...], CONTRACT_ROWS, preferred_element_type=F32)
        out_ref[:, base : base + grad_ref.shape[1]] = near_ref[...].astype(F32) + own
        base += grad_ref.shape[1]


def last_kernel(low_far_ref, high_far_ref, own_ref, after_ref, out_ref, out, sems):
    pieces = sems.shape[0]
    piece = out.shape[0] // pieces
    base = low_far_ref.shape[1]
    stores = []
    for k in range(pieces):
        rows = slice(k * piece, (k + 1) * piece)
        out[rows, :base] = (own_ref[rows, :base] + low_far_ref[rows, :].astype(F32)).astype(BF16)
        out[rows, base:] = (own_ref[rows, base:] + high_far_ref[rows, :].astype(F32)).astype(BF16)
        cut = pl.ds(k * piece, piece)
        stores.append(pltpu.make_async_copy(out.at[cut, :], out_ref.at[cut, :], sems.at[k]))
        stores[k].start()
    for store in stores:
        store.wait()


def sum_kernel(placed_ref, back_ref, after_ref, out_ref, token_ref, back, out, sems):
    pieces = sems.shape[1]
    piece = back.shape[1] // pieces
    loads, stores = [], []
    for k in range(pieces):
        cut = pl.ds(k * piece, piece)
        loads.append(pltpu.make_async_copy(back_ref.at[:, cut], back.at[:, cut], sems.at[0, k]))
        stores.append(pltpu.make_async_copy(out.at[:, cut], out_ref.at[:, cut], sems.at[1, k]))
        loads[k].start()
    for k in range(pieces):
        loads[k].wait()
        cut = slice(k * piece, (k + 1) * piece)
        out[:, cut] = jnp.dot(placed_ref[...], back[:, cut], preferred_element_type=F32).astype(BF16)
        stores[k].start()
    for store in stores:
        store.wait()
    token_ref[...] = jnp.zeros_like(token_ref)


def body(
    hidden,
    output_weight,
    owners,
    negatives,
    negative_mask,
    target_block,
    target_word,
    log_norm,
    cotangent,
):
    tokens, width = hidden.shape
    visits = owners.shape[1]
    peers = lax.axis_size("vocab")
    planes = lax.axis_size("dp")
    words = output_weight.shape[1]
    capacity = max(2, tokens * visits * 4 // (3 * peers))
    slots = peers * capacity
    sent = width + META
    chunk = width // planes
    base = LOW_BLOCKS * BLOCK
    def in_hbm(x):
        return pltpu.with_memory_space_constraint(x, pltpu.HBM)

    anywhere = pl.BlockSpec(memory_space=pl.ANY)
    hbm = pl.BlockSpec(memory_space=pltpu.HBM)
    vmem = pl.BlockSpec(memory_space=pltpu.VMEM)
    smem = pl.BlockSpec(memory_space=pltpu.SMEM)
    far = planes // 2
    near = far - 1

    def whole(*shape):
        return pl.BlockSpec(shape, lambda i: (0,) * len(shape))

    smalls = [
        owners.T,
        negatives.transpose(1, 2, 0),
        negative_mask.transpose(1, 2, 0),
        target_block[None, :],
        target_word[None, :],
        log_norm[None, :],
        cotangent[None, :],
    ]
    send, place = pl.pallas_call(
        functools.partial(place_kernel, capacity),
        grid=(1,),
        in_specs=[hbm] + [whole(*x.shape) for x in smalls],
        out_specs=[hbm, whole(slots, tokens)],
        out_shape=[
            pltpu.HBM((slots, sent), BF16),
            jax.ShapeDtypeStruct((slots, tokens), BF16),
        ],
        scratch_shapes=[
            pltpu.VMEM((tokens, width), BF16),
            pltpu.VMEM((slots, sent), BF16),
            pltpu.SemaphoreType.DMA((width // 512 + 1,)),
        ],
        compiler_params=params(24),
        cost_estimate=cost(0),
        name="place_rows",
    )(*[in_hbm(x) for x in (hidden, *smalls)])
    got = lax.all_to_all(
        send.reshape(peers, capacity, sent), "vocab", split_axis=0, concat_axis=0, tiled=True
    ).reshape(slots, sent)

    placed = pl.pallas_call(
        turn_kernel,
        in_specs=[vmem],
        out_specs=vmem,
        out_shape=jax.ShapeDtypeStruct((tokens, slots), BF16),
        cost_estimate=cost(100),
        compiler_params=params(4),
        name="turn_places",
    )(place)
    weights = in_hbm(output_weight)
    got = in_hbm(got)
    chunks = lax.rem(lax.axis_index("dp") + jnp.arange(planes, dtype=jnp.int32), planes)

    def like(*shape):
        return jax.ShapeDtypeStruct(shape, BF16)

    token = jax.ShapeDtypeStruct((8, 128), F32)
    depth = width // STEPS
    rest = words - base
    rows, meta, low_weight, high_weight, low, low_far, low_near = pl.pallas_call(
        low_kernel,
        in_specs=[smem, hbm, hbm, anywhere],
        out_specs=[vmem] * 7,
        out_shape=[
            like(slots, width),
            like(slots, META),
            like(STEPS, depth, base),
            like(STEPS, depth, rest),
            like(slots, base),
            like(chunk, base),
            like(chunk, base),
        ],
        scratch_shapes=[pltpu.VMEM((slots, base), F32), pltpu.SemaphoreType.DMA((4, STEPS))],
        compiler_params=params(24),
        cost_estimate=cost(0),
        name="low_scores",
    )(chunks, got, weights, placed)
    high, high_far, high_near = pl.pallas_call(
        functools.partial(high_kernel, base),
        in_specs=[smem, vmem, vmem, vmem],
        out_specs=[vmem] * 3,
        out_shape=[like(slots, rest), like(chunk, rest), like(chunk, rest)],
        scratch_shapes=[pltpu.VMEM((slots, rest), F32)],
        compiler_params=params(16),
        cost_estimate=cost(HIGH_US),
        name="high_scores",
    )(chunks, rows, meta, high_weight)

    def hop(x, d):
        return lax.ppermute(x, "dp", [(i, (i + d) % planes) for i in range(planes)])

    def rows_spec(k):
        return pl.BlockSpec((slots, chunk), lambda i, c: (0, c[k % planes]))

    def message_spec(some):
        return pl.BlockSpec((chunk, some), lambda i, c: (0, 0))

    token_spec = pl.BlockSpec((8, 128), lambda i, c: (0, 0))

    def state_parts(after):
        return pl.pallas_call(
            back_kernel,
            in_specs=[vmem, vmem, vmem, vmem, anywhere],
            out_specs=[hbm, vmem],
            out_shape=[pltpu.HBM((slots, width), BF16), token],
            scratch_shapes=[
                pltpu.VMEM((planes, slots, chunk), BF16),
                pltpu.SemaphoreType.DMA((planes,)),
            ],
            compiler_params=params(16),
            cost_estimate=cost(STATE_US),
            name="state_parts",
        )(low, high, low_weight, high_weight, after)

    def add(k, grad, arrived, after, us):
        some = grad.shape[1]
        return pl.pallas_call(
            add_kernel,
            grid_spec=pltpu.PrefetchScalarGridSpec(
                num_scalar_prefetch=1,
                grid=(1,),
                in_specs=[message_spec(some), rows_spec(k), message_spec(some), anywhere],
                out_specs=[message_spec(some), token_spec],
            ),
            out_shape=[like(chunk, some), token],
            compiler_params=params(12),
            cost_estimate=cost(us),
            name="add_part",
        )(chunks, arrived, got, grad, after)

    flows = [(1, low, far), (-1, low, near), (-1, high, far), (1, high, near)]
    messages = [low_far, low_near, high_far, high_near]
    after = high_near
    event = 0
    for step in range(far):
        for f, (d, grad, hops) in enumerate(flows):
            if step < hops:
                messages[f] = hop(messages[f], d)
                if step < hops - 1:
                    if event == GAP:
                        part, after = state_parts(after)
                    messages[f], after = add(
                        d * (hops - 1 - step), grad, messages[f], after, HOPS_US[event]
                    )
                    event += 1
    back = lax.all_to_all(
        part.reshape(peers, capacity, width), "vocab", split_axis=0, concat_axis=0, tiled=True
    ).reshape(slots, width)

    own, after = pl.pallas_call(
        own_kernel,
        grid_spec=pltpu.PrefetchScalarGridSpec(
            num_scalar_prefetch=1,
            grid=(1,),
            in_specs=[
                message_spec(base),
                message_spec(rest),
                rows_spec(0),
                message_spec(base),
                message_spec(rest),
                anywhere,
            ],
            out_specs=[pl.BlockSpec((chunk, words), lambda i, c: (0, 0)), token_spec],
        ),
        out_shape=[jax.ShapeDtypeStruct((chunk, words), F32), token],
        compiler_params=params(16),
        cost_estimate=cost(OWN_US),
        name="own_part",
    )(chunks, messages[1], messages[3], got, low, high, after)
    hidden_grad, after = pl.pallas_call(
        sum_kernel,
        in_specs=[vmem, hbm, anywhere],
        out_specs=[hbm, vmem],
        out_shape=[pltpu.HBM((tokens, width), BF16), token],
        scratch_shapes=[
            pltpu.VMEM((slots, width), BF16),
            pltpu.VMEM((tokens, width), BF16),
            pltpu.SemaphoreType.DMA((2, STEPS)),
        ],
        compiler_params=params(12),
        cost_estimate=cost(SUM_US),
        name="sum_parts",
    )(placed, in_hbm(back), after)
    weight_grad = pl.pallas_call(
        last_kernel,
        in_specs=[vmem, vmem, vmem, anywhere],
        out_specs=hbm,
        out_shape=pltpu.HBM((chunk, words), BF16),
        scratch_shapes=[pltpu.VMEM((chunk, words), BF16), pltpu.SemaphoreType.DMA((2,))],
        compiler_params=params(12),
        cost_estimate=cost(LAST_US),
        name="last_add",
    )(messages[0], messages[2], own, after)
    return (hidden_grad, weight_grad)


def solution(mesh):
    placed = (
        P(("dp", "vocab"), None),
        P(None, "vocab"),
        P(("dp", "vocab"), None),
        P(("dp", "vocab"), None, None),
        P(("dp", "vocab"), None, None),
        P(("dp", "vocab")),
        P(("dp", "vocab")),
        P(("dp", "vocab")),
        P(("dp", "vocab")),
    )
    return jax.shard_map(
        body,
        mesh=mesh,
        in_specs=placed,
        out_specs=(P(("dp", "vocab"), None), P("dp", "vocab")),
        check_vma=False,
    )
```

```python
import functools

import jax
import jax.numpy as jnp
from jax import lax
from jax.experimental import pallas as pl
from jax.experimental.pallas import tpu as pltpu
from jax.sharding import PartitionSpec as P

BLOCK = 128
BLK_DEV = 8
META = 128
GAP = 0
STEPS = 8
AHEAD = 2
LOW_BLOCKS = 5
MIB = 1 << 20
F32 = jnp.float32
BF16 = jnp.bfloat16
HOPS_US = (3,) * 10
OWN_US, SUM_US, HIGH_US, STATE_US, LAST_US = 100, 0, 0, 0, 0


def cost(us):
    return pl.CostEstimate(flops=int(us * 1.15e9), bytes_accessed=0, transcendentals=0)


CONTRACT_ROWS = (((0,), (0,)), ((), ()))
CONTRACT_COLS = (((1,), (1,)), ((), ()))


def params(mib):
    return pltpu.CompilerParams(vmem_limit_bytes=mib * MIB)


def place_kernel(
    capacity,
    hidden_ref,
    owners_ref,
    negatives_ref,
    mask_ref,
    block_ref,
    word_ref,
    norm_ref,
    cot_ref,
    send_ref,
    place_ref,
    hidden,
    send,
    sems,
):
    tokens, width = hidden_ref.shape
    load = pltpu.make_async_copy(hidden_ref, hidden, sems.at[width // 512])
    load.start()
    visits, picks = negatives_ref.shape[:2]
    slots = send_ref.shape[0]
    peers = slots // capacity
    owner_iota = lax.broadcasted_iota(jnp.int32, (peers, tokens), 0)
    row = lax.broadcasted_iota(jnp.int32, (tokens, tokens), 0)
    col = lax.broadcasted_iota(jnp.int32, (tokens, tokens), 1)
    before = jnp.where(row < col, 1.0, 0.0).astype(BF16)
    slot_iota = lax.broadcasted_iota(jnp.int32, (slots, tokens), 0)
    cluster = lax.broadcasted_iota(jnp.int32, (BLK_DEV, tokens), 0)
    carried = jnp.zeros((peers, 1), F32)
    block = block_ref[...]
    total = jnp.zeros((slots, tokens), F32)
    info = jnp.zeros((slots, META), F32)
    for v in range(visits):
        owner = owners_ref[v : v + 1, :]
        hot = jnp.where(owner_iota == owner, 1.0, 0.0)
        earlier = jnp.dot(hot.astype(BF16), before, preferred_element_type=F32) + carried
        carried = carried + jnp.sum(hot, axis=1, keepdims=True)
        position = jnp.sum(hot * earlier, axis=0, keepdims=True).astype(jnp.int32)
        place = jnp.where(slot_iota == owner * capacity + position, 1.0, 0.0)
        total = total + place
        counts = jnp.zeros((BLK_DEV, tokens), F32)
        for n in range(picks):
            used = mask_ref[v, n : n + 1, :] == 1
            counts += jnp.where((cluster == negatives_ref[v, n : n + 1, :]) & used, 1.0, 0.0)
        if v == 0:
            counts += jnp.where(cluster == block, 1.0, 0.0)
            here = block.astype(F32)
        else:
            here = jnp.full((1, tokens), -1.0, F32)
        tail = jnp.zeros((META - BLK_DEV - 4, tokens), F32)
        meta = jnp.concatenate(
            [
                counts,
                cot_ref[...].astype(F32),
                norm_ref[...].astype(F32),
                here,
                word_ref[...].astype(F32),
                tail,
            ],
            axis=0,
        ).astype(BF16)
        info += lax.dot_general(
            place.astype(BF16), meta, CONTRACT_COLS, preferred_element_type=F32
        )
    place_tokens = total.astype(BF16)
    place_ref[...] = place_tokens
    send[:, width:] = info.astype(BF16)
    step = 512
    load.wait()
    stores = []
    for k, c in enumerate(range(0, width, step)):
        send[:, c : c + step] = jnp.dot(
            place_tokens, hidden[:, c : c + step], preferred_element_type=F32
        ).astype(BF16)
        cut = pl.ds(c, step + META if c + step == width else step)
        stores.append(pltpu.make_async_copy(send.at[:, cut], send_ref.at[:, cut], sems.at[k]))
        stores[-1].start()
    for store in stores:
        store.wait()


def turn_kernel(place_ref, placed_ref):
    placed_ref[...] = place_ref[...].astype(F32).T.astype(BF16)


def score_half(base, chunks_ref, rows_ref, meta_ref, weight, grad_ref, far_ref, near_ref, acc, ready):
    steps, depth, half = weight.shape
    for k in range(steps):
        ready(k)
        part = jnp.dot(
            rows_ref[:, k * depth : (k + 1) * depth], weight[k], preferred_element_type=F32
        )
        if k == 0:
            acc[...] = part
        else:
            acc[...] += part
    ready(steps)
    info = meta_ref[...].astype(F32)
    lane = lax.broadcasted_iota(jnp.int32, (1, BLOCK), 1).astype(F32)
    scale = info[:, BLK_DEV : BLK_DEV + 1]
    norm = info[:, BLK_DEV + 1 : BLK_DEV + 2]
    target = info[:, BLK_DEV + 2 : BLK_DEV + 3] * BLOCK + info[:, BLK_DEV + 3 : BLK_DEV + 4]
    for b in range(half // BLOCK):
        first = base + b * BLOCK
        count = info[:, first // BLOCK : first // BLOCK + 1]
        words = slice(b * BLOCK, (b + 1) * BLOCK)
        soft = jnp.where(count > 0, count * jnp.exp(acc[:, words] - norm), 0.0)
        hit = jnp.where(lane + first == target, 1.0, 0.0)
        grad_ref[:, words] = (scale * (soft - hit)).astype(BF16)
    chunk = far_ref.shape[0]
    far = rows_ref.shape[1] // chunk // 2
    near = far - 1 if base else far + 1
    for k, out_ref in ((far, far_ref), (near, near_ref)):
        out_ref[...] = lax.dot_general(
            rows_ref[:, pl.ds(pl.multiple_of(chunks_ref[k] * chunk, chunk), chunk)],
            grad_ref[...],
            CONTRACT_ROWS,
            preferred_element_type=F32,
        ).astype(BF16)


def weight_loads(weight_ref, weight, sems, base):
    steps, depth, some = weight.shape
    return [
        pltpu.make_async_copy(
            weight_ref.at[pl.ds(k * depth, depth), pl.ds(base, some)], weight.at[k], sems.at[k]
        )
        for k in range(steps)
    ]


def low_kernel(
    chunks_ref,
    got_ref,
    weight_ref,
    after_ref,
    rows_ref,
    meta_ref,
    low_weight,
    high_weight,
    grad_ref,
    far_ref,
    near_ref,
    acc,
    sems,
):
    steps, depth, some = low_weight.shape
    weights = weight_loads(weight_ref, low_weight, sems.at[0], 0)
    others = weight_loads(weight_ref, high_weight, sems.at[1], some)
    loads = []
    for k in range(steps):
        cut = pl.ds(k * depth, depth)
        loads.append(pltpu.make_async_copy(got_ref.at[:, cut], rows_ref.at[:, cut], sems.at[2, k]))
    last = pltpu.make_async_copy(got_ref.at[:, pl.ds(steps * depth, META)], meta_ref, sems.at[3, 0])
    queue = [(weights[k], loads[k]) for k in range(steps)]
    queue[0] += (last,)
    queue += [(others[k], others[k + 1]) for k in range(0, steps, 2)]

    def start(k):
        for load in queue[k] if k < len(queue) else ():
            load.start()

    for k in range(AHEAD):
        start(k)

    def ready(k):
        if k == steps:
            for late in range(steps + AHEAD, len(queue)):
                start(late)
        else:
            for load in queue[k]:
                load.wait()
            start(k + AHEAD)

    score_half(0, chunks_ref, rows_ref, meta_ref, low_weight, grad_ref, far_ref, near_ref, acc, ready)
    for other in others:
        other.wait()


def high_kernel(base, chunks_ref, rows_ref, meta_ref, weight, grad_ref, far_ref, near_ref, acc):
    score_half(
        base, chunks_ref, rows_ref, meta_ref, weight, grad_ref, far_ref, near_ref, acc, lambda k: None
    )


def back_kernel(
    low_ref, high_ref, low_weight, high_weight, after_ref, part_ref, token_ref, part, sems
):
    steps, depth, _ = low_weight.shape
    pieces, _, piece = part.shape
    stores = []
    for k in range(pieces):
        step, place = divmod(k * piece, depth)
        cut = slice(place, place + piece)
        total = lax.dot_general(
            low_ref[...], low_weight[step, cut, :], CONTRACT_COLS, preferred_element_type=F32
        ) + lax.dot_general(
            high_ref[...], high_weight[step, cut, :], CONTRACT_COLS, preferred_element_type=F32
        )
        part[k] = total.astype(BF16)
        stores.append(
            pltpu.make_async_copy(part.at[k], part_ref.at[:, pl.ds(k * piece, piece)], sems.at[k])
        )
        stores[k].start()
    for store in stores:
        store.wait()
    token_ref[...] = jnp.zeros_like(token_ref)


def add_kernel(chunks_ref, got_ref, rows_ref, grad_ref, after_ref, out_ref, token_ref):
    own = lax.dot_general(rows_ref[...], grad_ref[...], CONTRACT_ROWS, preferred_element_type=F32)
    out_ref[...] = (got_ref[...].astype(F32) + own).astype(BF16)
    token_ref[...] = jnp.zeros_like(token_ref)


def own_kernel(
    chunks_ref, low_near_ref, high_near_ref, rows_ref, low_ref, high_ref, after_ref, out_ref, token_ref
):
    token_ref[...] = jnp.zeros_like(token_ref)
    base = 0
    for near_ref, grad_ref in ((low_near_ref, low_ref), (high_near_ref, high_ref)):
        own = lax.dot_general(rows_ref[...], grad_ref[...], CONTRACT_ROWS, preferred_element_type=F32)
        out_ref[:, base : base + grad_ref.shape[1]] = near_ref[...].astype(F32) + own
        base += grad_ref.shape[1]


def last_kernel(low_far_ref, high_far_ref, own_ref, after_ref, out_ref, out, sems):
    pieces = sems.shape[0]
    piece = out.shape[0] // pieces
    base = low_far_ref.shape[1]
    stores = []
    for k in range(pieces):
        rows = slice(k * piece, (k + 1) * piece)
        out[rows, :base] = (own_ref[rows, :base] + low_far_ref[rows, :].astype(F32)).astype(BF16)
        out[rows, base:] = (own_ref[rows, base:] + high_far_ref[rows, :].astype(F32)).astype(BF16)
        cut = pl.ds(k * piece, piece)
        stores.append(pltpu.make_async_copy(out.at[cut, :], out_ref.at[cut, :], sems.at[k]))
        stores[k].start()
    for store in stores:
        store.wait()


def sum_kernel(placed_ref, back_ref, after_ref, out_ref, token_ref, back, out, sems):
    pieces = sems.shape[1]
    piece = back.shape[1] // pieces
    loads, stores = [], []
    for k in range(pieces):
        cut = pl.ds(k * piece, piece)
        loads.append(pltpu.make_async_copy(back_ref.at[:, cut], back.at[:, cut], sems.at[0, k]))
        stores.append(pltpu.make_async_copy(out.at[:, cut], out_ref.at[:, cut], sems.at[1, k]))
        loads[k].start()
    for k in range(pieces):
        loads[k].wait()
        cut = slice(k * piece, (k + 1) * piece)
        out[:, cut] = jnp.dot(placed_ref[...], back[:, cut], preferred_element_type=F32).astype(BF16)
        stores[k].start()
    for store in stores:
        store.wait()
    token_ref[...] = jnp.zeros_like(token_ref)


def body(
    hidden,
    output_weight,
    owners,
    negatives,
    negative_mask,
    target_block,
    target_word,
    log_norm,
    cotangent,
):
    tokens, width = hidden.shape
    visits = owners.shape[1]
    peers = lax.axis_size("vocab")
    planes = lax.axis_size("dp")
    words = output_weight.shape[1]
    capacity = max(2, tokens * visits * 4 // (3 * peers))
    slots = peers * capacity
    sent = width + META
    chunk = width // planes
    base = LOW_BLOCKS * BLOCK
    def in_hbm(x):
        return pltpu.with_memory_space_constraint(x, pltpu.HBM)

    anywhere = pl.BlockSpec(memory_space=pl.ANY)
    hbm = pl.BlockSpec(memory_space=pltpu.HBM)
    vmem = pl.BlockSpec(memory_space=pltpu.VMEM)
    smem = pl.BlockSpec(memory_space=pltpu.SMEM)
    far = planes // 2
    near = far - 1

    def whole(*shape):
        return pl.BlockSpec(shape, lambda i: (0,) * len(shape))

    smalls = [
        owners.T,
        negatives.transpose(1, 2, 0),
        negative_mask.transpose(1, 2, 0),
        target_block[None, :],
        target_word[None, :],
        log_norm[None, :],
        cotangent[None, :],
    ]
    send, place = pl.pallas_call(
        functools.partial(place_kernel, capacity),
        grid=(1,),
        in_specs=[hbm] + [whole(*x.shape) for x in smalls],
        out_specs=[hbm, whole(slots, tokens)],
        out_shape=[
            pltpu.HBM((slots, sent), BF16),
            jax.ShapeDtypeStruct((slots, tokens), BF16),
        ],
        scratch_shapes=[
            pltpu.VMEM((tokens, width), BF16),
            pltpu.VMEM((slots, sent), BF16),
            pltpu.SemaphoreType.DMA((width // 512 + 1,)),
        ],
        compiler_params=params(24),
        cost_estimate=cost(0),
        name="place_rows",
    )(*[in_hbm(x) for x in (hidden, *smalls)])
    got = lax.all_to_all(
        send.reshape(peers, capacity, sent), "vocab", split_axis=0, concat_axis=0, tiled=True
    ).reshape(slots, sent)

    placed = pl.pallas_call(
        turn_kernel,
        in_specs=[vmem],
        out_specs=vmem,
        out_shape=jax.ShapeDtypeStruct((tokens, slots), BF16),
        cost_estimate=cost(100),
        compiler_params=params(4),
        name="turn_places",
    )(place)
    weights = in_hbm(output_weight)
    got = in_hbm(got)
    chunks = lax.rem(lax.axis_index("dp") + jnp.arange(planes, dtype=jnp.int32), planes)

    def like(*shape):
        return jax.ShapeDtypeStruct(shape, BF16)

    token = jax.ShapeDtypeStruct((8, 128), F32)
    depth = width // STEPS
    rest = words - base
    rows, meta, low_weight, high_weight, low, low_far, low_near = pl.pallas_call(
        low_kernel,
        in_specs=[smem, hbm, hbm, anywhere],
        out_specs=[vmem] * 7,
        out_shape=[
            like(slots, width),
            like(slots, META),
            like(STEPS, depth, base),
            like(STEPS, depth, rest),
            like(slots, base),
            like(chunk, base),
            like(chunk, base),
        ],
        scratch_shapes=[pltpu.VMEM((slots, base), F32), pltpu.SemaphoreType.DMA((4, STEPS))],
        compiler_params=params(24),
        cost_estimate=cost(0),
        name="low_scores",
    )(chunks, got, weights, placed)
    high, high_far, high_near = pl.pallas_call(
        functools.partial(high_kernel, base),
        in_specs=[smem, vmem, vmem, vmem],
        out_specs=[vmem] * 3,
        out_shape=[like(slots, rest), like(chunk, rest), like(chunk, rest)],
        scratch_shapes=[pltpu.VMEM((slots, rest), F32)],
        compiler_params=params(16),
        cost_estimate=cost(HIGH_US),
        name="high_scores",
    )(chunks, rows, meta, high_weight)

    def hop(x, d):
        return lax.ppermute(x, "dp", [(i, (i + d) % planes) for i in range(planes)])

    def rows_spec(k):
        return pl.BlockSpec((slots, chunk), lambda i, c: (0, c[k % planes]))

    def message_spec(some):
        return pl.BlockSpec((chunk, some), lambda i, c: (0, 0))

    token_spec = pl.BlockSpec((8, 128), lambda i, c: (0, 0))

    def state_parts(after):
        return pl.pallas_call(
            back_kernel,
            in_specs=[vmem, vmem, vmem, vmem, anywhere],
            out_specs=[hbm, vmem],
            out_shape=[pltpu.HBM((slots, width), BF16), token],
            scratch_shapes=[
                pltpu.VMEM((planes, slots, chunk), BF16),
                pltpu.SemaphoreType.DMA((planes,)),
            ],
            compiler_params=params(16),
            cost_estimate=cost(STATE_US),
            name="state_parts",
        )(low, high, low_weight, high_weight, after)

    def add(k, grad, arrived, after, us):
        some = grad.shape[1]
        return pl.pallas_call(
            add_kernel,
            grid_spec=pltpu.PrefetchScalarGridSpec(
                num_scalar_prefetch=1,
                grid=(1,),
                in_specs=[message_spec(some), rows_spec(k), message_spec(some), anywhere],
                out_specs=[message_spec(some), token_spec],
            ),
            out_shape=[like(chunk, some), token],
            compiler_params=params(12),
            cost_estimate=cost(us),
            name="add_part",
        )(chunks, arrived, got, grad, after)

    flows = [(1, low, far), (-1, low, near), (-1, high, far), (1, high, near)]
    messages = [low_far, low_near, high_far, high_near]
    after = high_near
    event = 0
    for step in range(far):
        for f, (d, grad, hops) in enumerate(flows):
            if step < hops:
                messages[f] = hop(messages[f], d)
                if step < hops - 1:
                    if event == GAP:
                        part, after = state_parts(after)
                    messages[f], after = add(
                        d * (hops - 1 - step), grad, messages[f], after, HOPS_US[event]
                    )
                    event += 1
    back = lax.all_to_all(
        part.reshape(peers, capacity, width), "vocab", split_axis=0, concat_axis=0, tiled=True
    ).reshape(slots, width)

    own, after = pl.pallas_call(
        own_kernel,
        grid_spec=pltpu.PrefetchScalarGridSpec(
            num_scalar_prefetch=1,
            grid=(1,),
            in_specs=[
                message_spec(base),
                message_spec(rest),
                rows_spec(0),
                message_spec(base),
                message_spec(rest),
                anywhere,
            ],
            out_specs=[pl.BlockSpec((chunk, words), lambda i, c: (0, 0)), token_spec],
        ),
        out_shape=[jax.ShapeDtypeStruct((chunk, words), F32), token],
        compiler_params=params(16),
        cost_estimate=cost(OWN_US),
        name="own_part",
    )(chunks, messages[1], messages[3], got, low, high, after)
    hidden_grad, after = pl.pallas_call(
        sum_kernel,
        in_specs=[vmem, hbm, anywhere],
        out_specs=[hbm, vmem],
        out_shape=[pltpu.HBM((tokens, width), BF16), token],
        scratch_shapes=[
            pltpu.VMEM((slots, width), BF16),
            pltpu.VMEM((tokens, width), BF16),
            pltpu.SemaphoreType.DMA((2, STEPS)),
        ],
        compiler_params=params(12),
        cost_estimate=cost(SUM_US),
        name="sum_parts",
    )(placed, in_hbm(back), after)
    weight_grad = pl.pallas_call(
        last_kernel,
        in_specs=[vmem, vmem, vmem, anywhere],
        out_specs=hbm,
        out_shape=pltpu.HBM((chunk, words), BF16),
        scratch_shapes=[pltpu.VMEM((chunk, words), BF16), pltpu.SemaphoreType.DMA((2,))],
        compiler_params=params(12),
        cost_estimate=cost(LAST_US),
        name="last_add",
    )(messages[0], messages[2], own, after)
    return (hidden_grad, weight_grad)


def solution(mesh):
    placed = (
        P(("dp", "vocab"), None),
        P(None, "vocab"),
        P(("dp", "vocab"), None),
        P(("dp", "vocab"), None, None),
        P(("dp", "vocab"), None, None),
        P(("dp", "vocab")),
        P(("dp", "vocab")),
        P(("dp", "vocab")),
        P(("dp", "vocab")),
    )
    return jax.shard_map(
        body,
        mesh=mesh,
        in_specs=placed,
        out_specs=(P(("dp", "vocab"), None), P("dp", "vocab")),
        check_vma=False,
    )
```

```python
import functools

import jax
import jax.numpy as jnp
from jax import lax
from jax.experimental import pallas as pl
from jax.experimental.pallas import tpu as pltpu
from jax.sharding import PartitionSpec as P

BLOCK = 128
BLK_DEV = 8
META = 128
GAP = 2
STEPS = 4
LOW_BLOCKS = 4
MIB = 1 << 20
F32 = jnp.float32
BF16 = jnp.bfloat16
HOPS_US = (3, 3, 3, 3, 3, 3, 3, 3, 30, 30)
SUM_US, HIGH_US, STATE_US, LAST_US = 0, 2, 4, 20


def cost(us):
    return pl.CostEstimate(flops=int(us * 1.15e9), bytes_accessed=0, transcendentals=0)


CONTRACT_ROWS = (((0,), (0,)), ((), ()))
CONTRACT_COLS = (((1,), (1,)), ((), ()))


def params(mib):
    return pltpu.CompilerParams(vmem_limit_bytes=mib * MIB)


def place_kernel(
    capacity,
    hidden_ref,
    owners_ref,
    negatives_ref,
    mask_ref,
    block_ref,
    word_ref,
    norm_ref,
    cot_ref,
    send_ref,
    place_ref,
    hidden,
    send,
    sems,
):
    tokens, width = hidden_ref.shape
    load = pltpu.make_async_copy(hidden_ref, hidden, sems.at[width // 512])
    load.start()
    visits, picks = negatives_ref.shape[:2]
    slots = send_ref.shape[0]
    peers = slots // capacity
    owner_iota = lax.broadcasted_iota(jnp.int32, (peers, tokens), 0)
    row = lax.broadcasted_iota(jnp.int32, (tokens, tokens), 0)
    col = lax.broadcasted_iota(jnp.int32, (tokens, tokens), 1)
    before = jnp.where(row < col, 1.0, 0.0).astype(BF16)
    slot_iota = lax.broadcasted_iota(jnp.int32, (slots, tokens), 0)
    cluster = lax.broadcasted_iota(jnp.int32, (BLK_DEV, tokens), 0)
    carried = jnp.zeros((peers, 1), F32)
    block = block_ref[...]
    total = jnp.zeros((slots, tokens), F32)
    info = jnp.zeros((slots, META), F32)
    for v in range(visits):
        owner = owners_ref[v : v + 1, :]
        hot = jnp.where(owner_iota == owner, 1.0, 0.0)
        earlier = jnp.dot(hot.astype(BF16), before, preferred_element_type=F32) + carried
        carried = carried + jnp.sum(hot, axis=1, keepdims=True)
        position = jnp.sum(hot * earlier, axis=0, keepdims=True).astype(jnp.int32)
        place = jnp.where(slot_iota == owner * capacity + position, 1.0, 0.0)
        total = total + place
        counts = jnp.zeros((BLK_DEV, tokens), F32)
        for n in range(picks):
            used = mask_ref[v, n : n + 1, :] == 1
            counts += jnp.where((cluster == negatives_ref[v, n : n + 1, :]) & used, 1.0, 0.0)
        if v == 0:
            counts += jnp.where(cluster == block, 1.0, 0.0)
            here = block.astype(F32)
        else:
            here = jnp.full((1, tokens), -1.0, F32)
        tail = jnp.zeros((META - BLK_DEV - 4, tokens), F32)
        meta = jnp.concatenate(
            [
                counts,
                cot_ref[...].astype(F32),
                norm_ref[...].astype(F32),
                here,
                word_ref[...].astype(F32),
                tail,
            ],
            axis=0,
        ).astype(BF16)
        info += lax.dot_general(
            place.astype(BF16), meta, CONTRACT_COLS, preferred_element_type=F32
        )
    place_tokens = total.astype(BF16)
    place_ref[...] = place_tokens
    send[:, width:] = info.astype(BF16)
    step = 512
    load.wait()
    stores = []
    for k, c in enumerate(range(0, width, step)):
        send[:, c : c + step] = jnp.dot(
            place_tokens, hidden[:, c : c + step], preferred_element_type=F32
        ).astype(BF16)
        cut = pl.ds(c, step + META if c + step == width else step)
        stores.append(pltpu.make_async_copy(send.at[:, cut], send_ref.at[:, cut], sems.at[k]))
        stores[-1].start()
    for store in stores:
        store.wait()


def turn_kernel(place_ref, placed_ref):
    placed_ref[...] = place_ref[...].astype(F32).T.astype(BF16)


def score_half(base, chunks_ref, rows_ref, meta_ref, weight, grad_ref, far_ref, near_ref, acc, ready):
    steps, depth, half = weight.shape
    for k in range(steps):
        ready(k)
        part = jnp.dot(
            rows_ref[:, k * depth : (k + 1) * depth], weight[k], preferred_element_type=F32
        )
        if k == 0:
            acc[...] = part
        else:
            acc[...] += part
    ready(steps)
    info = meta_ref[...].astype(F32)
    lane = lax.broadcasted_iota(jnp.int32, (1, BLOCK), 1).astype(F32)
    scale = info[:, BLK_DEV : BLK_DEV + 1]
    norm = info[:, BLK_DEV + 1 : BLK_DEV + 2]
    target = info[:, BLK_DEV + 2 : BLK_DEV + 3] * BLOCK + info[:, BLK_DEV + 3 : BLK_DEV + 4]
    for b in range(half // BLOCK):
        first = base + b * BLOCK
        count = info[:, first // BLOCK : first // BLOCK + 1]
        words = slice(b * BLOCK, (b + 1) * BLOCK)
        soft = jnp.where(count > 0, count * jnp.exp(acc[:, words] - norm), 0.0)
        hit = jnp.where(lane + first == target, 1.0, 0.0)
        grad_ref[:, words] = (scale * (soft - hit)).astype(BF16)
    chunk = far_ref.shape[0]
    far = rows_ref.shape[1] // chunk // 2
    near = far - 1 if base else far + 1
    for k, out_ref in ((far, far_ref), (near, near_ref)):
        out_ref[...] = lax.dot_general(
            rows_ref[:, pl.ds(pl.multiple_of(chunks_ref[k] * chunk, chunk), chunk)],
            grad_ref[...],
            CONTRACT_ROWS,
            preferred_element_type=F32,
        ).astype(BF16)


def weight_loads(weight_ref, weight, sems, base):
    steps, depth, some = weight.shape
    return [
        pltpu.make_async_copy(
            weight_ref.at[pl.ds(k * depth, depth), pl.ds(base, some)], weight.at[k], sems.at[k]
        )
        for k in range(steps)
    ]


def low_kernel(
    chunks_ref,
    got_ref,
    weight_ref,
    after_ref,
    rows_ref,
    meta_ref,
    low_weight,
    grad_ref,
    far_ref,
    near_ref,
    acc,
    sems,
):
    steps, depth, _ = low_weight.shape
    weights = weight_loads(weight_ref, low_weight, sems.at[0], 0)
    loads = []
    for k in range(steps):
        cut = pl.ds(k * depth, depth)
        loads.append(pltpu.make_async_copy(got_ref.at[:, cut], rows_ref.at[:, cut], sems.at[2, k]))
    last = pltpu.make_async_copy(got_ref.at[:, pl.ds(steps * depth, META)], meta_ref, sems.at[3, 0])
    for k in range(steps):
        weights[k].start()
        loads[k].start()
    last.start()

    def ready(k):
        if k == steps:
            last.wait()
        else:
            weights[k].wait()
            loads[k].wait()

    score_half(0, chunks_ref, rows_ref, meta_ref, low_weight, grad_ref, far_ref, near_ref, acc, ready)


def high_kernel(
    base, chunks_ref, rows_ref, meta_ref, weight_ref, weight, grad_ref, far_ref, near_ref, acc, sems
):
    loads = weight_loads(weight_ref, weight, sems, base)
    for load in loads:
        load.start()

    def ready(k):
        if k < len(loads):
            loads[k].wait()

    score_half(base, chunks_ref, rows_ref, meta_ref, weight, grad_ref, far_ref, near_ref, acc, ready)


def back_kernel(
    low_ref, high_ref, low_weight, high_weight, after_ref, part_ref, token_ref, part, sems
):
    steps, depth, _ = low_weight.shape
    pieces, _, piece = part.shape
    stores = []
    for k in range(pieces):
        step, place = divmod(k * piece, depth)
        cut = slice(place, place + piece)
        total = lax.dot_general(
            low_ref[...], low_weight[step, cut, :], CONTRACT_COLS, preferred_element_type=F32
        ) + lax.dot_general(
            high_ref[...], high_weight[step, cut, :], CONTRACT_COLS, preferred_element_type=F32
        )
        part[k] = total.astype(BF16)
        stores.append(
            pltpu.make_async_copy(part.at[k], part_ref.at[:, pl.ds(k * piece, piece)], sems.at[k])
        )
        stores[k].start()
    for store in stores:
        store.wait()
    token_ref[...] = jnp.zeros_like(token_ref)


def add_kernel(chunks_ref, got_ref, rows_ref, grad_ref, after_ref, out_ref, token_ref):
    own = lax.dot_general(rows_ref[...], grad_ref[...], CONTRACT_ROWS, preferred_element_type=F32)
    out_ref[...] = (got_ref[...].astype(F32) + own).astype(BF16)
    token_ref[...] = jnp.zeros_like(token_ref)


def last_kernel(
    chunks_ref,
    low_far_ref,
    low_near_ref,
    high_far_ref,
    high_near_ref,
    got_ref,
    low_ref,
    high_ref,
    after_ref,
    out_ref,
    rows,
    out,
    sems,
):
    chunk, base = low_far_ref.shape
    cut = pl.ds(pl.multiple_of(chunks_ref[0] * chunk, chunk), chunk)
    load = pltpu.make_async_copy(got_ref.at[:, cut], rows, sems.at[2])
    load.start()
    load.wait()
    stores = []
    for k, (far_ref, near_ref, grad_ref, words) in enumerate(
        (
            (low_far_ref, low_near_ref, low_ref, slice(0, base)),
            (high_far_ref, high_near_ref, high_ref, slice(base, out.shape[1])),
        )
    ):
        own = lax.dot_general(rows[...], grad_ref[...], CONTRACT_ROWS, preferred_element_type=F32)
        out[:, words] = (own + (far_ref[...].astype(F32) + near_ref[...].astype(F32))).astype(BF16)
        cut = pl.ds(words.start, words.stop - words.start)
        stores.append(pltpu.make_async_copy(out.at[:, cut], out_ref.at[:, cut], sems.at[k]))
        stores[k].start()
    for store in stores:
        store.wait()


def sum_kernel(placed_ref, back_ref, after_ref, out_ref, token_ref, back, out, sems):
    pieces = sems.shape[1]
    piece = back.shape[1] // pieces
    loads, stores = [], []
    for k in range(pieces):
        cut = pl.ds(k * piece, piece)
        loads.append(pltpu.make_async_copy(back_ref.at[:, cut], back.at[:, cut], sems.at[0, k]))
        stores.append(pltpu.make_async_copy(out.at[:, cut], out_ref.at[:, cut], sems.at[1, k]))
        loads[k].start()
    for k in range(pieces):
        loads[k].wait()
        cut = slice(k * piece, (k + 1) * piece)
        out[:, cut] = jnp.dot(placed_ref[...], back[:, cut], preferred_element_type=F32).astype(BF16)
        stores[k].start()
    for store in stores:
        store.wait()
    token_ref[...] = jnp.zeros_like(token_ref)


def body(
    hidden,
    output_weight,
    owners,
    negatives,
    negative_mask,
    target_block,
    target_word,
    log_norm,
    cotangent,
):
    tokens, width = hidden.shape
    visits = owners.shape[1]
    peers = lax.axis_size("vocab")
    planes = lax.axis_size("dp")
    words = output_weight.shape[1]
    capacity = max(2, tokens * visits * 4 // (3 * peers))
    slots = peers * capacity
    sent = width + META
    chunk = width // planes
    base = LOW_BLOCKS * BLOCK
    def in_hbm(x):
        return pltpu.with_memory_space_constraint(x, pltpu.HBM)

    anywhere = pl.BlockSpec(memory_space=pl.ANY)
    hbm = pl.BlockSpec(memory_space=pltpu.HBM)
    vmem = pl.BlockSpec(memory_space=pltpu.VMEM)
    smem = pl.BlockSpec(memory_space=pltpu.SMEM)
    far = planes // 2
    near = far - 1

    def whole(*shape):
        return pl.BlockSpec(shape, lambda i: (0,) * len(shape))

    smalls = [
        owners.T,
        negatives.transpose(1, 2, 0),
        negative_mask.transpose(1, 2, 0),
        target_block[None, :],
        target_word[None, :],
        log_norm[None, :],
        cotangent[None, :],
    ]
    send, place = pl.pallas_call(
        functools.partial(place_kernel, capacity),
        grid=(1,),
        in_specs=[hbm] + [whole(*x.shape) for x in smalls],
        out_specs=[hbm, whole(slots, tokens)],
        out_shape=[
            pltpu.HBM((slots, sent), BF16),
            jax.ShapeDtypeStruct((slots, tokens), BF16),
        ],
        scratch_shapes=[
            pltpu.VMEM((tokens, width), BF16),
            pltpu.VMEM((slots, sent), BF16),
            pltpu.SemaphoreType.DMA((width // 512 + 1,)),
        ],
        compiler_params=params(24),
        cost_estimate=cost(0),
        name="place_rows",
    )(*[in_hbm(x) for x in (hidden, *smalls)])
    got = lax.all_to_all(
        send.reshape(peers, capacity, sent), "vocab", split_axis=0, concat_axis=0, tiled=True
    ).reshape(slots, sent)

    placed = pl.pallas_call(
        turn_kernel,
        in_specs=[vmem],
        out_specs=vmem,
        out_shape=jax.ShapeDtypeStruct((tokens, slots), BF16),
        cost_estimate=cost(100),
        compiler_params=params(4),
        name="turn_places",
    )(place)
    weights = in_hbm(output_weight)
    got = in_hbm(got)
    chunks = lax.rem(lax.axis_index("dp") + jnp.arange(planes, dtype=jnp.int32), planes)

    def like(*shape):
        return jax.ShapeDtypeStruct(shape, BF16)

    token = jax.ShapeDtypeStruct((8, 128), F32)
    depth = width // STEPS
    rest = words - base
    rows, meta, low_weight, low, low_far, low_near = pl.pallas_call(
        low_kernel,
        in_specs=[smem, hbm, hbm, anywhere],
        out_specs=[vmem] * 6,
        out_shape=[
            like(slots, width),
            like(slots, META),
            like(STEPS, depth, base),
            like(slots, base),
            like(chunk, base),
            like(chunk, base),
        ],
        scratch_shapes=[pltpu.VMEM((slots, base), F32), pltpu.SemaphoreType.DMA((4, STEPS))],
        compiler_params=params(24),
        cost_estimate=cost(0),
        name="low_scores",
    )(chunks, got, weights, placed)
    high_weight, high, high_far, high_near = pl.pallas_call(
        functools.partial(high_kernel, base),
        in_specs=[smem, vmem, vmem, hbm],
        out_specs=[vmem] * 4,
        out_shape=[like(STEPS, depth, rest), like(slots, rest), like(chunk, rest), like(chunk, rest)],
        scratch_shapes=[pltpu.VMEM((slots, rest), F32), pltpu.SemaphoreType.DMA((STEPS,))],
        compiler_params=params(16),
        cost_estimate=cost(HIGH_US),
        name="high_scores",
    )(chunks, rows, meta, weights)

    def hop(x, d):
        return lax.ppermute(x, "dp", [(i, (i + d) % planes) for i in range(planes)])

    def rows_spec(k):
        return pl.BlockSpec((slots, chunk), lambda i, c: (0, c[k % planes]))

    def message_spec(some):
        return pl.BlockSpec((chunk, some), lambda i, c: (0, 0))

    token_spec = pl.BlockSpec((8, 128), lambda i, c: (0, 0))

    def state_parts(after):
        return pl.pallas_call(
            back_kernel,
            in_specs=[vmem, vmem, vmem, vmem, anywhere],
            out_specs=[hbm, vmem],
            out_shape=[pltpu.HBM((slots, width), BF16), token],
            scratch_shapes=[
                pltpu.VMEM((planes, slots, chunk), BF16),
                pltpu.SemaphoreType.DMA((planes,)),
            ],
            compiler_params=params(16),
            cost_estimate=cost(STATE_US),
            name="state_parts",
        )(low, high, low_weight, high_weight, after)

    def add(k, grad, arrived, after, us):
        some = grad.shape[1]
        return pl.pallas_call(
            add_kernel,
            grid_spec=pltpu.PrefetchScalarGridSpec(
                num_scalar_prefetch=1,
                grid=(1,),
                in_specs=[message_spec(some), rows_spec(k), message_spec(some), anywhere],
                out_specs=[message_spec(some), token_spec],
            ),
            out_shape=[like(chunk, some), token],
            compiler_params=params(12),
            cost_estimate=cost(us),
            name="add_part",
        )(chunks, arrived, got, grad, after)

    flows = [(1, low, far), (-1, low, near), (-1, high, far), (1, high, near)]
    messages = [low_far, low_near, high_far, high_near]
    after = high_near
    event = 0
    for step in range(far):
        for f, (d, grad, hops) in enumerate(flows):
            if step < hops:
                messages[f] = hop(messages[f], d)
                if step < hops - 1:
                    if event == GAP:
                        part, after = state_parts(after)
                    messages[f], after = add(
                        d * (hops - 1 - step), grad, messages[f], after, HOPS_US[event]
                    )
                    event += 1
    back = lax.all_to_all(
        part.reshape(peers, capacity, width), "vocab", split_axis=0, concat_axis=0, tiled=True
    ).reshape(slots, width)

    hidden_grad, after = pl.pallas_call(
        sum_kernel,
        in_specs=[vmem, hbm, anywhere],
        out_specs=[hbm, vmem],
        out_shape=[pltpu.HBM((tokens, width), BF16), token],
        scratch_shapes=[
            pltpu.VMEM((slots, width), BF16),
            pltpu.VMEM((tokens, width), BF16),
            pltpu.SemaphoreType.DMA((2, STEPS)),
        ],
        compiler_params=params(12),
        cost_estimate=cost(SUM_US),
        name="sum_parts",
    )(placed, in_hbm(back), after)
    weight_grad = pl.pallas_call(
        last_kernel,
        in_specs=[smem] + [vmem] * 4 + [hbm, vmem, vmem, anywhere],
        out_specs=hbm,
        out_shape=pltpu.HBM((chunk, words), BF16),
        scratch_shapes=[
            pltpu.VMEM((slots, chunk), BF16),
            pltpu.VMEM((chunk, words), BF16),
            pltpu.SemaphoreType.DMA((3,)),
        ],
        compiler_params=params(12),
        cost_estimate=cost(LAST_US),
        name="last_add",
    )(chunks, messages[0], messages[1], messages[2], messages[3], got, low, high, after)
    return (hidden_grad, weight_grad)


def solution(mesh):
    placed = (
        P(("dp", "vocab"), None),
        P(None, "vocab"),
        P(("dp", "vocab"), None),
        P(("dp", "vocab"), None, None),
        P(("dp", "vocab"), None, None),
        P(("dp", "vocab")),
        P(("dp", "vocab")),
        P(("dp", "vocab")),
        P(("dp", "vocab")),
    )
    return jax.shard_map(
        body,
        mesh=mesh,
        in_specs=placed,
        out_specs=(P(("dp", "vocab"), None), P("dp", "vocab")),
        check_vma=False,
    )
```

```python
import functools

import jax
import jax.numpy as jnp
from jax import lax
from jax.experimental import pallas as pl
from jax.experimental.pallas import tpu as pltpu
from jax.sharding import PartitionSpec as P

BLOCK = 128
BLK_DEV = 8
META = 128
GAP = 1
STEPS = 4
LOW_BLOCKS = 5
MIB = 1 << 20
F32 = jnp.float32
BF16 = jnp.bfloat16
HOPS_US = (3,) * 10
OWN_US, SUM_US, HIGH_US, STATE_US, LAST_US = 100, 0, 0, 0, 0


def cost(us):
    return pl.CostEstimate(flops=int(us * 1.15e9), bytes_accessed=0, transcendentals=0)


CONTRACT_ROWS = (((0,), (0,)), ((), ()))
CONTRACT_COLS = (((1,), (1,)), ((), ()))


def params(mib):
    return pltpu.CompilerParams(vmem_limit_bytes=mib * MIB)


def place_kernel(
    capacity,
    hidden_ref,
    owners_ref,
    negatives_ref,
    mask_ref,
    block_ref,
    word_ref,
    norm_ref,
    cot_ref,
    send_ref,
    place_ref,
    hidden,
    send,
    sems,
):
    tokens, width = hidden_ref.shape
    load = pltpu.make_async_copy(hidden_ref, hidden, sems.at[width // 512])
    load.start()
    visits, picks = negatives_ref.shape[:2]
    slots = send_ref.shape[0]
    peers = slots // capacity
    owner_iota = lax.broadcasted_iota(jnp.int32, (peers, tokens), 0)
    row = lax.broadcasted_iota(jnp.int32, (tokens, tokens), 0)
    col = lax.broadcasted_iota(jnp.int32, (tokens, tokens), 1)
    before = jnp.where(row < col, 1.0, 0.0).astype(BF16)
    slot_iota = lax.broadcasted_iota(jnp.int32, (slots, tokens), 0)
    cluster = lax.broadcasted_iota(jnp.int32, (BLK_DEV, tokens), 0)
    carried = jnp.zeros((peers, 1), F32)
    block = block_ref[...]
    total = jnp.zeros((slots, tokens), F32)
    info = jnp.zeros((slots, META), F32)
    for v in range(visits):
        owner = owners_ref[v : v + 1, :]
        hot = jnp.where(owner_iota == owner, 1.0, 0.0)
        earlier = jnp.dot(hot.astype(BF16), before, preferred_element_type=F32) + carried
        carried = carried + jnp.sum(hot, axis=1, keepdims=True)
        position = jnp.sum(hot * earlier, axis=0, keepdims=True).astype(jnp.int32)
        place = jnp.where(slot_iota == owner * capacity + position, 1.0, 0.0)
        total = total + place
        counts = jnp.zeros((BLK_DEV, tokens), F32)
        for n in range(picks):
            used = mask_ref[v, n : n + 1, :] == 1
            counts += jnp.where((cluster == negatives_ref[v, n : n + 1, :]) & used, 1.0, 0.0)
        if v == 0:
            counts += jnp.where(cluster == block, 1.0, 0.0)
            here = block.astype(F32)
        else:
            here = jnp.full((1, tokens), -1.0, F32)
        tail = jnp.zeros((META - BLK_DEV - 4, tokens), F32)
        meta = jnp.concatenate(
            [
                counts,
                cot_ref[...].astype(F32),
                norm_ref[...].astype(F32),
                here,
                word_ref[...].astype(F32),
                tail,
            ],
            axis=0,
        ).astype(BF16)
        info += lax.dot_general(
            place.astype(BF16), meta, CONTRACT_COLS, preferred_element_type=F32
        )
    place_tokens = total.astype(BF16)
    place_ref[...] = place_tokens
    send[:, width:] = info.astype(BF16)
    step = 512
    load.wait()
    stores = []
    for k, c in enumerate(range(0, width, step)):
        send[:, c : c + step] = jnp.dot(
            place_tokens, hidden[:, c : c + step], preferred_element_type=F32
        ).astype(BF16)
        cut = pl.ds(c, step + META if c + step == width else step)
        stores.append(pltpu.make_async_copy(send.at[:, cut], send_ref.at[:, cut], sems.at[k]))
        stores[-1].start()
    for store in stores:
        store.wait()


def turn_kernel(place_ref, placed_ref):
    placed_ref[...] = place_ref[...].astype(F32).T.astype(BF16)


def score_half(base, chunks_ref, rows_ref, meta_ref, weight, grad_ref, far_ref, near_ref, acc, ready):
    steps, depth, half = weight.shape
    for k in range(steps):
        ready(k)
        part = jnp.dot(
            rows_ref[:, k * depth : (k + 1) * depth], weight[k], preferred_element_type=F32
        )
        if k == 0:
            acc[...] = part
        else:
            acc[...] += part
    ready(steps)
    info = meta_ref[...].astype(F32)
    lane = lax.broadcasted_iota(jnp.int32, (1, BLOCK), 1).astype(F32)
    scale = info[:, BLK_DEV : BLK_DEV + 1]
    norm = info[:, BLK_DEV + 1 : BLK_DEV + 2]
    target = info[:, BLK_DEV + 2 : BLK_DEV + 3] * BLOCK + info[:, BLK_DEV + 3 : BLK_DEV + 4]
    for b in range(half // BLOCK):
        first = base + b * BLOCK
        count = info[:, first // BLOCK : first // BLOCK + 1]
        words = slice(b * BLOCK, (b + 1) * BLOCK)
        soft = jnp.where(count > 0, count * jnp.exp(acc[:, words] - norm), 0.0)
        hit = jnp.where(lane + first == target, 1.0, 0.0)
        grad_ref[:, words] = (scale * (soft - hit)).astype(BF16)
    chunk = far_ref.shape[0]
    far = rows_ref.shape[1] // chunk // 2
    near = far - 1 if base else far + 1
    for k, out_ref in ((far, far_ref), (near, near_ref)):
        out_ref[...] = lax.dot_general(
            rows_ref[:, pl.ds(pl.multiple_of(chunks_ref[k] * chunk, chunk), chunk)],
            grad_ref[...],
            CONTRACT_ROWS,
            preferred_element_type=F32,
        ).astype(BF16)


def weight_loads(weight_ref, weight, sems, base):
    steps, depth, some = weight.shape
    return [
        pltpu.make_async_copy(
            weight_ref.at[pl.ds(k * depth, depth), pl.ds(base, some)], weight.at[k], sems.at[k]
        )
        for k in range(steps)
    ]


def low_kernel(
    chunks_ref,
    got_ref,
    weight_ref,
    after_ref,
    rows_ref,
    meta_ref,
    low_weight,
    grad_ref,
    far_ref,
    near_ref,
    acc,
    sems,
):
    steps, depth, _ = low_weight.shape
    weights = weight_loads(weight_ref, low_weight, sems.at[0], 0)
    loads = []
    for k in range(steps):
        cut = pl.ds(k * depth, depth)
        loads.append(pltpu.make_async_copy(got_ref.at[:, cut], rows_ref.at[:, cut], sems.at[2, k]))
    last = pltpu.make_async_copy(got_ref.at[:, pl.ds(steps * depth, META)], meta_ref, sems.at[3, 0])
    for k in range(steps):
        weights[k].start()
        loads[k].start()
    last.start()

    def ready(k):
        if k == steps:
            last.wait()
        else:
            weights[k].wait()
            loads[k].wait()

    score_half(0, chunks_ref, rows_ref, meta_ref, low_weight, grad_ref, far_ref, near_ref, acc, ready)


def high_kernel(
    base, chunks_ref, rows_ref, meta_ref, weight_ref, weight, grad_ref, far_ref, near_ref, acc, sems
):
    loads = weight_loads(weight_ref, weight, sems, base)
    for load in loads:
        load.start()

    def ready(k):
        if k < len(loads):
            loads[k].wait()

    score_half(base, chunks_ref, rows_ref, meta_ref, weight, grad_ref, far_ref, near_ref, acc, ready)


def back_kernel(
    low_ref, high_ref, low_weight, high_weight, after_ref, part_ref, token_ref, part, sems
):
    steps, depth, _ = low_weight.shape
    pieces, _, piece = part.shape
    stores = []
    for k in range(pieces):
        step, place = divmod(k * piece, depth)
        cut = slice(place, place + piece)
        total = lax.dot_general(
            low_ref[...], low_weight[step, cut, :], CONTRACT_COLS, preferred_element_type=F32
        ) + lax.dot_general(
            high_ref[...], high_weight[step, cut, :], CONTRACT_COLS, preferred_element_type=F32
        )
        part[k] = total.astype(BF16)
        stores.append(
            pltpu.make_async_copy(part.at[k], part_ref.at[:, pl.ds(k * piece, piece)], sems.at[k])
        )
        stores[k].start()
    for store in stores:
        store.wait()
    token_ref[...] = jnp.zeros_like(token_ref)


def add_kernel(chunks_ref, got_ref, rows_ref, grad_ref, after_ref, out_ref, token_ref):
    own = lax.dot_general(rows_ref[...], grad_ref[...], CONTRACT_ROWS, preferred_element_type=F32)
    out_ref[...] = (got_ref[...].astype(F32) + own).astype(BF16)
    token_ref[...] = jnp.zeros_like(token_ref)


def own_kernel(
    chunks_ref, low_near_ref, high_near_ref, rows_ref, low_ref, high_ref, after_ref, out_ref, token_ref
):
    token_ref[...] = jnp.zeros_like(token_ref)
    base = 0
    for near_ref, grad_ref in ((low_near_ref, low_ref), (high_near_ref, high_ref)):
        own = lax.dot_general(rows_ref[...], grad_ref[...], CONTRACT_ROWS, preferred_element_type=F32)
        out_ref[:, base : base + grad_ref.shape[1]] = near_ref[...].astype(F32) + own
        base += grad_ref.shape[1]


def last_kernel(low_far_ref, high_far_ref, own_ref, after_ref, out_ref, out, sems):
    pieces = sems.shape[0]
    piece = out.shape[0] // pieces
    base = low_far_ref.shape[1]
    stores = []
    for k in range(pieces):
        rows = slice(k * piece, (k + 1) * piece)
        out[rows, :base] = (own_ref[rows, :base] + low_far_ref[rows, :].astype(F32)).astype(BF16)
        out[rows, base:] = (own_ref[rows, base:] + high_far_ref[rows, :].astype(F32)).astype(BF16)
        cut = pl.ds(k * piece, piece)
        stores.append(pltpu.make_async_copy(out.at[cut, :], out_ref.at[cut, :], sems.at[k]))
        stores[k].start()
    for store in stores:
        store.wait()


def sum_kernel(placed_ref, back_ref, after_ref, out_ref, token_ref, back, out, sems):
    pieces = sems.shape[1]
    piece = back.shape[1] // pieces
    loads, stores = [], []
    for k in range(pieces):
        cut = pl.ds(k * piece, piece)
        loads.append(pltpu.make_async_copy(back_ref.at[:, cut], back.at[:, cut], sems.at[0, k]))
        stores.append(pltpu.make_async_copy(out.at[:, cut], out_ref.at[:, cut], sems.at[1, k]))
        loads[k].start()
    for k in range(pieces):
        loads[k].wait()
        cut = slice(k * piece, (k + 1) * piece)
        out[:, cut] = jnp.dot(placed_ref[...], back[:, cut], preferred_element_type=F32).astype(BF16)
        stores[k].start()
    for store in stores:
        store.wait()
    token_ref[...] = jnp.zeros_like(token_ref)


def body(
    hidden,
    output_weight,
    owners,
    negatives,
    negative_mask,
    target_block,
    target_word,
    log_norm,
    cotangent,
):
    tokens, width = hidden.shape
    visits = owners.shape[1]
    peers = lax.axis_size("vocab")
    planes = lax.axis_size("dp")
    words = output_weight.shape[1]
    capacity = max(2, tokens * visits * 4 // (3 * peers))
    slots = peers * capacity
    sent = width + META
    chunk = width // planes
    base = LOW_BLOCKS * BLOCK
    def in_hbm(x):
        return pltpu.with_memory_space_constraint(x, pltpu.HBM)

    anywhere = pl.BlockSpec(memory_space=pl.ANY)
    hbm = pl.BlockSpec(memory_space=pltpu.HBM)
    vmem = pl.BlockSpec(memory_space=pltpu.VMEM)
    smem = pl.BlockSpec(memory_space=pltpu.SMEM)
    far = planes // 2
    near = far - 1

    def whole(*shape):
        return pl.BlockSpec(shape, lambda i: (0,) * len(shape))

    smalls = [
        owners.T,
        negatives.transpose(1, 2, 0),
        negative_mask.transpose(1, 2, 0),
        target_block[None, :],
        target_word[None, :],
        log_norm[None, :],
        cotangent[None, :],
    ]
    send, place = pl.pallas_call(
        functools.partial(place_kernel, capacity),
        grid=(1,),
        in_specs=[hbm] + [whole(*x.shape) for x in smalls],
        out_specs=[hbm, whole(slots, tokens)],
        out_shape=[
            pltpu.HBM((slots, sent), BF16),
            jax.ShapeDtypeStruct((slots, tokens), BF16),
        ],
        scratch_shapes=[
            pltpu.VMEM((tokens, width), BF16),
            pltpu.VMEM((slots, sent), BF16),
            pltpu.SemaphoreType.DMA((width // 512 + 1,)),
        ],
        compiler_params=params(24),
        cost_estimate=cost(0),
        name="place_rows",
    )(*[in_hbm(x) for x in (hidden, *smalls)])
    got = lax.all_to_all(
        send.reshape(peers, capacity, sent), "vocab", split_axis=0, concat_axis=0, tiled=True
    ).reshape(slots, sent)

    placed = pl.pallas_call(
        turn_kernel,
        in_specs=[vmem],
        out_specs=vmem,
        out_shape=jax.ShapeDtypeStruct((tokens, slots), BF16),
        cost_estimate=cost(100),
        compiler_params=params(4),
        name="turn_places",
    )(place)
    weights = in_hbm(output_weight)
    got = in_hbm(got)
    chunks = lax.rem(lax.axis_index("dp") + jnp.arange(planes, dtype=jnp.int32), planes)

    def like(*shape):
        return jax.ShapeDtypeStruct(shape, BF16)

    token = jax.ShapeDtypeStruct((8, 128), F32)
    depth = width // STEPS
    rest = words - base
    rows, meta, low_weight, low, low_far, low_near = pl.pallas_call(
        low_kernel,
        in_specs=[smem, hbm, hbm, anywhere],
        out_specs=[vmem] * 6,
        out_shape=[
            like(slots, width),
            like(slots, META),
            like(STEPS, depth, base),
            like(slots, base),
            like(chunk, base),
            like(chunk, base),
        ],
        scratch_shapes=[pltpu.VMEM((slots, base), F32), pltpu.SemaphoreType.DMA((4, STEPS))],
        compiler_params=params(24),
        cost_estimate=cost(0),
        name="low_scores",
    )(chunks, got, weights, placed)
    high_weight, high, high_far, high_near = pl.pallas_call(
        functools.partial(high_kernel, base),
        in_specs=[smem, vmem, vmem, hbm],
        out_specs=[vmem] * 4,
        out_shape=[like(STEPS, depth, rest), like(slots, rest), like(chunk, rest), like(chunk, rest)],
        scratch_shapes=[pltpu.VMEM((slots, rest), F32), pltpu.SemaphoreType.DMA((STEPS,))],
        compiler_params=params(16),
        cost_estimate=cost(HIGH_US),
        name="high_scores",
    )(chunks, rows, meta, weights)

    def hop(x, d):
        return lax.ppermute(x, "dp", [(i, (i + d) % planes) for i in range(planes)])

    def rows_spec(k):
        return pl.BlockSpec((slots, chunk), lambda i, c: (0, c[k % planes]))

    def message_spec(some):
        return pl.BlockSpec((chunk, some), lambda i, c: (0, 0))

    token_spec = pl.BlockSpec((8, 128), lambda i, c: (0, 0))

    def state_parts(after):
        return pl.pallas_call(
            back_kernel,
            in_specs=[vmem, vmem, vmem, vmem, anywhere],
            out_specs=[hbm, vmem],
            out_shape=[pltpu.HBM((slots, width), BF16), token],
            scratch_shapes=[
                pltpu.VMEM((planes, slots, chunk), BF16),
                pltpu.SemaphoreType.DMA((planes,)),
            ],
            compiler_params=params(16),
            cost_estimate=cost(STATE_US),
            name="state_parts",
        )(low, high, low_weight, high_weight, after)

    def add(k, grad, arrived, after, us):
        some = grad.shape[1]
        return pl.pallas_call(
            add_kernel,
            grid_spec=pltpu.PrefetchScalarGridSpec(
                num_scalar_prefetch=1,
                grid=(1,),
                in_specs=[message_spec(some), rows_spec(k), message_spec(some), anywhere],
                out_specs=[message_spec(some), token_spec],
            ),
            out_shape=[like(chunk, some), token],
            compiler_params=params(12),
            cost_estimate=cost(us),
            name="add_part",
        )(chunks, arrived, got, grad, after)

    flows = [(1, low, far), (-1, low, near), (-1, high, far), (1, high, near)]
    messages = [low_far, low_near, high_far, high_near]
    after = high_near
    event = 0
    for step in range(far):
        for f, (d, grad, hops) in enumerate(flows):
            if step < hops:
                messages[f] = hop(messages[f], d)
                if step < hops - 1:
                    if event == GAP:
                        part, after = state_parts(after)
                    messages[f], after = add(
                        d * (hops - 1 - step), grad, messages[f], after, HOPS_US[event]
                    )
                    event += 1
    back = lax.all_to_all(
        part.reshape(peers, capacity, width), "vocab", split_axis=0, concat_axis=0, tiled=True
    ).reshape(slots, width)

    own, after = pl.pallas_call(
        own_kernel,
        grid_spec=pltpu.PrefetchScalarGridSpec(
            num_scalar_prefetch=1,
            grid=(1,),
            in_specs=[
                message_spec(base),
                message_spec(rest),
                rows_spec(0),
                message_spec(base),
                message_spec(rest),
                anywhere,
            ],
            out_specs=[pl.BlockSpec((chunk, words), lambda i, c: (0, 0)), token_spec],
        ),
        out_shape=[jax.ShapeDtypeStruct((chunk, words), F32), token],
        compiler_params=params(16),
        cost_estimate=cost(OWN_US),
        name="own_part",
    )(chunks, messages[1], messages[3], got, low, high, after)
    hidden_grad, after = pl.pallas_call(
        sum_kernel,
        in_specs=[vmem, hbm, anywhere],
        out_specs=[hbm, vmem],
        out_shape=[pltpu.HBM((tokens, width), BF16), token],
        scratch_shapes=[
            pltpu.VMEM((slots, width), BF16),
            pltpu.VMEM((tokens, width), BF16),
            pltpu.SemaphoreType.DMA((2, STEPS)),
        ],
        compiler_params=params(12),
        cost_estimate=cost(SUM_US),
        name="sum_parts",
    )(placed, in_hbm(back), after)
    weight_grad = pl.pallas_call(
        last_kernel,
        in_specs=[vmem, vmem, vmem, anywhere],
        out_specs=hbm,
        out_shape=pltpu.HBM((chunk, words), BF16),
        scratch_shapes=[pltpu.VMEM((chunk, words), BF16), pltpu.SemaphoreType.DMA((2,))],
        compiler_params=params(12),
        cost_estimate=cost(LAST_US),
        name="last_add",
    )(messages[0], messages[2], own, after)
    return (hidden_grad, weight_grad)


def solution(mesh):
    placed = (
        P(("dp", "vocab"), None),
        P(None, "vocab"),
        P(("dp", "vocab"), None),
        P(("dp", "vocab"), None, None),
        P(("dp", "vocab"), None, None),
        P(("dp", "vocab")),
        P(("dp", "vocab")),
        P(("dp", "vocab")),
        P(("dp", "vocab")),
    )
    return jax.shard_map(
        body,
        mesh=mesh,
        in_specs=placed,
        out_specs=(P(("dp", "vocab"), None), P("dp", "vocab")),
        check_vma=False,
    )
```

```python
import functools

import jax
import jax.numpy as jnp
from jax import lax
from jax.experimental import pallas as pl
from jax.experimental.pallas import tpu as pltpu
from jax.sharding import PartitionSpec as P

BLOCK = 128
BLK_DEV = 8
META = 128
GAP = 0
STEPS = 4
MIB = 1 << 20
F32 = jnp.float32
BF16 = jnp.bfloat16
HOPS_US = (3,) * 10
OWN_US, SUM_US, LATE_US = 100, 0, 0


def cost(us):
    return pl.CostEstimate(flops=int(us * 1.15e9), bytes_accessed=0, transcendentals=0)


CONTRACT_ROWS = (((0,), (0,)), ((), ()))
CONTRACT_COLS = (((1,), (1,)), ((), ()))


def params(mib):
    return pltpu.CompilerParams(vmem_limit_bytes=mib * MIB)


def place_kernel(
    capacity,
    hidden_ref,
    owners_ref,
    negatives_ref,
    mask_ref,
    block_ref,
    word_ref,
    norm_ref,
    cot_ref,
    send_ref,
    place_ref,
    hidden,
    send,
    sems,
):
    tokens, width = hidden_ref.shape
    load = pltpu.make_async_copy(hidden_ref, hidden, sems.at[width // 512])
    load.start()
    visits, picks = negatives_ref.shape[:2]
    slots = send_ref.shape[0]
    peers = slots // capacity
    owner_iota = lax.broadcasted_iota(jnp.int32, (peers, tokens), 0)
    row = lax.broadcasted_iota(jnp.int32, (tokens, tokens), 0)
    col = lax.broadcasted_iota(jnp.int32, (tokens, tokens), 1)
    before = jnp.where(row < col, 1.0, 0.0).astype(BF16)
    slot_iota = lax.broadcasted_iota(jnp.int32, (slots, tokens), 0)
    cluster = lax.broadcasted_iota(jnp.int32, (BLK_DEV, tokens), 0)
    carried = jnp.zeros((peers, 1), F32)
    block = block_ref[...]
    total = jnp.zeros((slots, tokens), F32)
    info = jnp.zeros((slots, META), F32)
    for v in range(visits):
        owner = owners_ref[v : v + 1, :]
        hot = jnp.where(owner_iota == owner, 1.0, 0.0)
        earlier = jnp.dot(hot.astype(BF16), before, preferred_element_type=F32) + carried
        carried = carried + jnp.sum(hot, axis=1, keepdims=True)
        position = jnp.sum(hot * earlier, axis=0, keepdims=True).astype(jnp.int32)
        place = jnp.where(slot_iota == owner * capacity + position, 1.0, 0.0)
        total = total + place
        counts = jnp.zeros((BLK_DEV, tokens), F32)
        for n in range(picks):
            used = mask_ref[v, n : n + 1, :] == 1
            counts += jnp.where((cluster == negatives_ref[v, n : n + 1, :]) & used, 1.0, 0.0)
        if v == 0:
            counts += jnp.where(cluster == block, 1.0, 0.0)
            here = block.astype(F32)
        else:
            here = jnp.full((1, tokens), -1.0, F32)
        tail = jnp.zeros((META - BLK_DEV - 4, tokens), F32)
        meta = jnp.concatenate(
            [
                counts,
                cot_ref[...].astype(F32),
                norm_ref[...].astype(F32),
                here,
                word_ref[...].astype(F32),
                tail,
            ],
            axis=0,
        ).astype(BF16)
        info += lax.dot_general(
            place.astype(BF16), meta, CONTRACT_COLS, preferred_element_type=F32
        )
    place_tokens = total.astype(BF16)
    place_ref[...] = place_tokens
    send[:, width:] = info.astype(BF16)
    step = 512
    load.wait()
    stores = []
    for k, c in enumerate(range(0, width, step)):
        send[:, c : c + step] = jnp.dot(
            place_tokens, hidden[:, c : c + step], preferred_element_type=F32
        ).astype(BF16)
        cut = pl.ds(c, step + META if c + step == width else step)
        stores.append(pltpu.make_async_copy(send.at[:, cut], send_ref.at[:, cut], sems.at[k]))
        stores[-1].start()
    for store in stores:
        store.wait()


def turn_kernel(place_ref, placed_ref):
    placed_ref[...] = place_ref[...].astype(F32).T.astype(BF16)


def score_half(high, chunks_ref, rows_ref, meta_ref, weight, grad_ref, far_ref, near_ref, acc, ready):
    steps, depth, half = weight.shape
    base = high * half
    for k in range(steps):
        ready(k)
        part = jnp.dot(
            rows_ref[:, k * depth : (k + 1) * depth], weight[k], preferred_element_type=F32
        )
        if k == 0:
            acc[...] = part
        else:
            acc[...] += part
    ready(steps)
    info = meta_ref[...].astype(F32)
    lane = lax.broadcasted_iota(jnp.int32, (1, BLOCK), 1).astype(F32)
    scale = info[:, BLK_DEV : BLK_DEV + 1]
    norm = info[:, BLK_DEV + 1 : BLK_DEV + 2]
    target = info[:, BLK_DEV + 2 : BLK_DEV + 3] * BLOCK + info[:, BLK_DEV + 3 : BLK_DEV + 4]
    for b in range(half // BLOCK):
        first = base + b * BLOCK
        count = info[:, first // BLOCK : first // BLOCK + 1]
        words = slice(b * BLOCK, (b + 1) * BLOCK)
        soft = jnp.where(count > 0, count * jnp.exp(acc[:, words] - norm), 0.0)
        hit = jnp.where(lane + first == target, 1.0, 0.0)
        grad_ref[:, words] = (scale * (soft - hit)).astype(BF16)
    chunk = far_ref.shape[0]
    far = rows_ref.shape[1] // chunk // 2
    near = far - 1 if high else far + 1
    for k, out_ref in ((far, far_ref), (near, near_ref)):
        out_ref[...] = lax.dot_general(
            rows_ref[:, pl.ds(pl.multiple_of(chunks_ref[k] * chunk, chunk), chunk)],
            grad_ref[...],
            CONTRACT_ROWS,
            preferred_element_type=F32,
        ).astype(BF16)


def weight_loads(weight_ref, weight, sems, base):
    steps, depth, half = weight.shape
    return [
        pltpu.make_async_copy(
            weight_ref.at[pl.ds(k * depth, depth), pl.ds(base, half)], weight.at[k], sems.at[0, k]
        )
        for k in range(steps)
    ]


def low_kernel(
    chunks_ref, got_ref, weight_ref, after_ref, rows_ref, meta_ref, grad_ref, far_ref, near_ref, weight, acc, sems
):
    steps, depth, _ = weight.shape
    weights = weight_loads(weight_ref, weight, sems, 0)
    loads = []
    for k in range(steps):
        cut = pl.ds(k * depth, depth)
        loads.append(pltpu.make_async_copy(got_ref.at[:, cut], rows_ref.at[:, cut], sems.at[1, k]))
    last = pltpu.make_async_copy(got_ref.at[:, pl.ds(steps * depth, META)], meta_ref, sems.at[0, steps])
    for k in range(steps):
        weights[k].start()
        loads[k].start()
    last.start()

    def ready(k):
        if k == steps:
            last.wait()
        else:
            weights[k].wait()
            loads[k].wait()

    score_half(0, chunks_ref, rows_ref, meta_ref, weight, grad_ref, far_ref, near_ref, acc, ready)


def high_kernel(
    chunks_ref, rows_ref, meta_ref, weight_ref, grad_ref, far_ref, near_ref, weight, acc, sems
):
    loads = weight_loads(weight_ref, weight, sems, weight.shape[2])
    for load in loads:
        load.start()

    def ready(k):
        if k < len(loads):
            loads[k].wait()

    score_half(1, chunks_ref, rows_ref, meta_ref, weight, grad_ref, far_ref, near_ref, acc, ready)


def back_kernel(low_ref, high_ref, weight_ref, after_ref, part_ref, token_ref, grad, weight, part, sems):
    steps, depth, _ = weight.shape
    half = low_ref.shape[1]
    loads = [
        pltpu.make_async_copy(weight_ref.at[pl.ds(k * depth, depth), :], weight.at[k], sems.at[0, k])
        for k in range(steps)
    ]
    stores = [
        pltpu.make_async_copy(part.at[k], part_ref.at[:, pl.ds(k * depth, depth)], sems.at[1, k])
        for k in range(steps)
    ]
    for load in loads:
        load.start()
    grad[:, :half] = low_ref[...]
    grad[:, half:] = high_ref[...]
    for k in range(steps):
        loads[k].wait()
        part[k] = lax.dot_general(
            grad[...], weight[k], CONTRACT_COLS, preferred_element_type=F32
        ).astype(BF16)
        stores[k].start()
    for store in stores:
        store.wait()
    token_ref[...] = jnp.zeros_like(token_ref)


def add_kernel(chunks_ref, got_ref, rows_ref, grad_ref, after_ref, out_ref, token_ref):
    own = lax.dot_general(rows_ref[...], grad_ref[...], CONTRACT_ROWS, preferred_element_type=F32)
    out_ref[...] = (got_ref[...].astype(F32) + own).astype(BF16)
    token_ref[...] = jnp.zeros_like(token_ref)


def own_kernel(chunks_ref, low_near_ref, high_near_ref, rows_ref, low_ref, high_ref, after_ref, out_ref, token_ref):
    half = low_ref.shape[1]
    token_ref[...] = jnp.zeros_like(token_ref)
    for k, near_ref, grad_ref in ((0, low_near_ref, low_ref), (1, high_near_ref, high_ref)):
        own = lax.dot_general(rows_ref[...], grad_ref[...], CONTRACT_ROWS, preferred_element_type=F32)
        out_ref[:, k * half : (k + 1) * half] = near_ref[...].astype(F32) + own


def last_kernel(low_far_ref, high_far_ref, own_ref, after_ref, out_ref, out, sems):
    pieces = sems.shape[0]
    piece = out.shape[0] // pieces
    base = low_far_ref.shape[1]
    stores = []
    for k in range(pieces):
        rows = slice(k * piece, (k + 1) * piece)
        out[rows, :base] = (own_ref[rows, :base] + low_far_ref[rows, :].astype(F32)).astype(BF16)
        out[rows, base:] = (own_ref[rows, base:] + high_far_ref[rows, :].astype(F32)).astype(BF16)
        cut = pl.ds(k * piece, piece)
        stores.append(pltpu.make_async_copy(out.at[cut, :], out_ref.at[cut, :], sems.at[k]))
        stores[k].start()
    for store in stores:
        store.wait()


def sum_kernel(placed_ref, back_ref, after_ref, out_ref, token_ref, back, out, sems):
    pieces = sems.shape[1]
    piece = back.shape[1] // pieces
    loads, stores = [], []
    for k in range(pieces):
        cut = pl.ds(k * piece, piece)
        loads.append(pltpu.make_async_copy(back_ref.at[:, cut], back.at[:, cut], sems.at[0, k]))
        stores.append(pltpu.make_async_copy(out.at[:, cut], out_ref.at[:, cut], sems.at[1, k]))
        loads[k].start()
    for k in range(pieces):
        loads[k].wait()
        cut = slice(k * piece, (k + 1) * piece)
        out[:, cut] = jnp.dot(placed_ref[...], back[:, cut], preferred_element_type=F32).astype(BF16)
        stores[k].start()
    for store in stores:
        store.wait()
    token_ref[...] = jnp.zeros_like(token_ref)


def body(
    hidden,
    output_weight,
    owners,
    negatives,
    negative_mask,
    target_block,
    target_word,
    log_norm,
    cotangent,
):
    tokens, width = hidden.shape
    visits = owners.shape[1]
    peers = lax.axis_size("vocab")
    planes = lax.axis_size("dp")
    words = output_weight.shape[1]
    capacity = max(2, tokens * visits * 4 // (3 * peers))
    slots = peers * capacity
    sent = width + META
    chunk = width // planes
    half = words // 2
    def in_hbm(x):
        return pltpu.with_memory_space_constraint(x, pltpu.HBM)

    anywhere = pl.BlockSpec(memory_space=pl.ANY)
    hbm = pl.BlockSpec(memory_space=pltpu.HBM)
    vmem = pl.BlockSpec(memory_space=pltpu.VMEM)
    smem = pl.BlockSpec(memory_space=pltpu.SMEM)
    far = planes // 2
    near = far - 1

    def whole(*shape):
        return pl.BlockSpec(shape, lambda i: (0,) * len(shape))

    smalls = [
        owners.T,
        negatives.transpose(1, 2, 0),
        negative_mask.transpose(1, 2, 0),
        target_block[None, :],
        target_word[None, :],
        log_norm[None, :],
        cotangent[None, :],
    ]
    send, place = pl.pallas_call(
        functools.partial(place_kernel, capacity),
        grid=(1,),
        in_specs=[hbm] + [whole(*x.shape) for x in smalls],
        out_specs=[hbm, whole(slots, tokens)],
        out_shape=[
            pltpu.HBM((slots, sent), BF16),
            jax.ShapeDtypeStruct((slots, tokens), BF16),
        ],
        scratch_shapes=[
            pltpu.VMEM((tokens, width), BF16),
            pltpu.VMEM((slots, sent), BF16),
            pltpu.SemaphoreType.DMA((width // 512 + 1,)),
        ],
        compiler_params=params(24),
        cost_estimate=cost(0),
        name="place_rows",
    )(*[in_hbm(x) for x in (hidden, *smalls)])
    got = lax.all_to_all(
        send.reshape(peers, capacity, sent), "vocab", split_axis=0, concat_axis=0, tiled=True
    ).reshape(slots, sent)

    placed = pl.pallas_call(
        turn_kernel,
        in_specs=[vmem],
        out_specs=vmem,
        out_shape=jax.ShapeDtypeStruct((tokens, slots), BF16),
        cost_estimate=cost(100),
        compiler_params=params(4),
        name="turn_places",
    )(place)
    weights = in_hbm(output_weight)
    got = in_hbm(got)
    chunks = lax.rem(lax.axis_index("dp") + jnp.arange(planes, dtype=jnp.int32), planes)

    message = jax.ShapeDtypeStruct((chunk, half), BF16)
    grad_half = jax.ShapeDtypeStruct((slots, half), BF16)
    token = jax.ShapeDtypeStruct((8, 128), F32)
    acc = pltpu.VMEM((slots, half), F32)
    half_weight = pltpu.VMEM((STEPS, width // STEPS, half), BF16)
    rows, meta, low, low_far, low_near = pl.pallas_call(
        low_kernel,
        in_specs=[smem, hbm, hbm, anywhere],
        out_specs=[vmem] * 5,
        out_shape=[
            jax.ShapeDtypeStruct((slots, width), BF16),
            jax.ShapeDtypeStruct((slots, META), BF16),
            grad_half,
            message,
            message,
        ],
        scratch_shapes=[half_weight, acc, pltpu.SemaphoreType.DMA((2, STEPS + 1))],
        compiler_params=params(20),
        cost_estimate=cost(0),
        name="low_scores",
    )(chunks, got, weights, placed)
    high, high_far, high_near = pl.pallas_call(
        high_kernel,
        in_specs=[smem, vmem, vmem, hbm],
        out_specs=[vmem] * 3,
        out_shape=[grad_half, message, message],
        scratch_shapes=[half_weight, acc, pltpu.SemaphoreType.DMA((1, STEPS))],
        compiler_params=params(20),
        cost_estimate=cost(LATE_US),
        name="high_scores",
    )(chunks, rows, meta, weights)

    def hop(x, d):
        return lax.ppermute(x, "dp", [(i, (i + d) % planes) for i in range(planes)])

    def rows_spec(k):
        return pl.BlockSpec((slots, chunk), lambda i, c: (0, c[k % planes]))

    message_spec = pl.BlockSpec((chunk, half), lambda i, c: (0, 0))
    token_spec = pl.BlockSpec((8, 128), lambda i, c: (0, 0))

    def state_parts(after):
        return pl.pallas_call(
            back_kernel,
            in_specs=[vmem, vmem, hbm, anywhere],
            out_specs=[hbm, vmem],
            out_shape=[pltpu.HBM((slots, width), BF16), token],
            scratch_shapes=[
                pltpu.VMEM((slots, words), BF16),
                pltpu.VMEM((planes, chunk, words), BF16),
                pltpu.VMEM((planes, slots, chunk), BF16),
                pltpu.SemaphoreType.DMA((2, planes)),
            ],
            compiler_params=params(24),
            cost_estimate=cost(LATE_US),
            name="state_parts",
        )(low, high, weights, after)

    def add(k, grad, arrived, after, us):
        return pl.pallas_call(
            add_kernel,
            grid_spec=pltpu.PrefetchScalarGridSpec(
                num_scalar_prefetch=1,
                grid=(1,),
                in_specs=[message_spec, rows_spec(k), message_spec, anywhere],
                out_specs=[message_spec, token_spec],
            ),
            out_shape=[message, token],
            compiler_params=params(12),
            cost_estimate=cost(us),
            name="add_part",
        )(chunks, arrived, got, grad, after)

    flows = [(1, low, far), (-1, low, near), (-1, high, far), (1, high, near)]
    messages = [low_far, low_near, high_far, high_near]
    after = high_near
    event = 0
    for step in range(far):
        for f, (d, grad, hops) in enumerate(flows):
            if step < hops:
                messages[f] = hop(messages[f], d)
                if step < hops - 1:
                    if event == GAP:
                        part, after = state_parts(after)
                    messages[f], after = add(
                        d * (hops - 1 - step), grad, messages[f], after, HOPS_US[event]
                    )
                    event += 1
    back = lax.all_to_all(
        part.reshape(peers, capacity, width), "vocab", split_axis=0, concat_axis=0, tiled=True
    ).reshape(slots, width)

    own, after = pl.pallas_call(
        own_kernel,
        grid_spec=pltpu.PrefetchScalarGridSpec(
            num_scalar_prefetch=1,
            grid=(1,),
            in_specs=[message_spec] * 2 + [rows_spec(0)] + [message_spec] * 2 + [anywhere],
            out_specs=[pl.BlockSpec((chunk, words), lambda i, c: (0, 0)), token_spec],
        ),
        out_shape=[jax.ShapeDtypeStruct((chunk, words), F32), token],
        compiler_params=params(16),
        cost_estimate=cost(OWN_US),
        name="own_part",
    )(chunks, messages[1], messages[3], got, low, high, after)
    hidden_grad, after = pl.pallas_call(
        sum_kernel,
        in_specs=[vmem, hbm, anywhere],
        out_specs=[hbm, vmem],
        out_shape=[pltpu.HBM((tokens, width), BF16), token],
        scratch_shapes=[
            pltpu.VMEM((slots, width), BF16),
            pltpu.VMEM((tokens, width), BF16),
            pltpu.SemaphoreType.DMA((2, STEPS)),
        ],
        compiler_params=params(12),
        cost_estimate=cost(SUM_US),
        name="sum_parts",
    )(placed, in_hbm(back), after)
    weight_grad = pl.pallas_call(
        last_kernel,
        in_specs=[vmem, vmem, vmem, anywhere],
        out_specs=hbm,
        out_shape=pltpu.HBM((chunk, words), BF16),
        scratch_shapes=[pltpu.VMEM((chunk, words), BF16), pltpu.SemaphoreType.DMA((2,))],
        compiler_params=params(12),
        cost_estimate=cost(0),
        name="last_add",
    )(messages[0], messages[2], own, after)
    return (hidden_grad, weight_grad)


def solution(mesh):
    placed = (
        P(("dp", "vocab"), None),
        P(None, "vocab"),
        P(("dp", "vocab"), None),
        P(("dp", "vocab"), None, None),
        P(("dp", "vocab"), None, None),
        P(("dp", "vocab")),
        P(("dp", "vocab")),
        P(("dp", "vocab")),
        P(("dp", "vocab")),
    )
    return jax.shard_map(
        body,
        mesh=mesh,
        in_specs=placed,
        out_specs=(P(("dp", "vocab"), None), P("dp", "vocab")),
        check_vma=False,
    )
```
